256 devices in a mesh: row: 64 (over z, y, x_lo), col: 4 (over x_hi, core).
Axes of the slice: x: 4 (x_hi: 2, x_lo: 2; x = x_hi * 2 + x_lo), y: 4, z: 8, core: 2. Of those that a mesh axis runs over, the one named last changes fastest.
Arguments:
- moments: float32 [1536, 2, 16, 1536], P('row', None, None, 'col'), may hold values from 0.1 to 2.5
Outputs:
- first_y: float32 [1536, 2, 16, 1536], P('row', None, None, 'col')
- second_y: float32 [1536, 2, 16, 1536], P('row', None, None, 'col')
- first_z: float32 [1536, 2, 16, 1536], P('row', None, None, 'col')
- second_z: float32 [1536, 2, 16, 1536], P('row', None, None, 'col')
The draws below stay inside these ranges and needn't reach their ends.
All inputs are finite; a program needn't handle non-finite values.
Results may differ from the reference program's by a relative error of at most 0.00013.
Values sent between devices are 32-bit elements; how exact they have to be, the bound alone decides.
No kernel may reach another device: no remote copies, remote signals or barrier semaphores. Data moves between devices by JAX's collectives and lax.ppermute only.
A program may use at most 128 MiB of HBM per device.

```python
import math
import jax
import jax.numpy as jnp

NX = 16
NY = 1536
NZ = 1536


def level_of(rng, extent, shards, least, largest):
    factor_of, own = 1.0, jax.random.fold_in(rng, 6)
    for dim, blocks in shards:
        steps = jnp.exp(jax.random.uniform(jax.random.fold_in(own, dim), (blocks,), jnp.float32, least / len(shards), largest / len(shards)))
        factor_of = factor_of * jnp.repeat(steps, extent[dim] // blocks).reshape([-1 if axis == dim else 1 for axis in range(len(extent))])
    return factor_of


def setup_inputs(seed: int = 0) -> dict:
    key_list = jax.random.split(jax.random.key(seed), 2)
    moments = jnp.clip(jnp.exp(math.log(2.5) - 3.218876 * jax.random.uniform(key_list[0], (NY, 2, NX, NZ), jnp.float32) ** level_of(key_list[0], (NY, 2, NX, NZ), ((0, 64), (3, 4)), -0.2, 0.2)), 0.1, 2.5)
    return dict(moments=moments)


def spectral_pair(values_in, axis_index):
    length = values_in.shape[axis_index]
    spectrum = jnp.fft.rfft(values_in, axis=axis_index)
    mode_index = jnp.arange(length // 2 + 1, dtype=jnp.float32)
    wavenumber = mode_index * (2.0 * jnp.pi / length)
    keep_mask = jnp.where(mode_index < length // 2, 1.0, 0.0).astype(jnp.float32)
    layout = [1] * values_in.ndim
    layout[axis_index] = length // 2 + 1
    wavenumber = wavenumber.reshape(layout)
    keep_mask = keep_mask.reshape(layout)
    first_out = jnp.fft.irfft(spectrum * (1j * wavenumber * keep_mask), n=length, axis=axis_index)
    second_out = jnp.fft.irfft(spectrum * (-(wavenumber * wavenumber)), n=length, axis=axis_index)
    return first_out.astype(jnp.float32), second_out.astype(jnp.float32)


def reference(moments):
    first_y, second_y = spectral_pair(moments, 0)
    first_z, second_z = spectral_pair(moments, 3)
    return first_y, second_y, first_z, second_z
```

```python
import math

import jax
import jax.numpy as jnp
import ml_dtypes
import numpy as np
from jax import lax
from jax.experimental import pallas as pl
from jax.experimental.pallas import tpu as pltpu
from jax.sharding import Mesh
from jax.sharding import PartitionSpec as P

COUNT = 1536
HALF = COUNT // 2
QUARTER = COUNT // 4
ROWS = 24
LANES = 384
PLANES = 32
F32 = jnp.float32
BF16 = jnp.bfloat16


def kernels():
    k = np.arange(COUNT, dtype=np.float64)
    sign = np.where(np.arange(COUNT) % 2 == 0, 1.0, -1.0)
    angle = math.pi * np.where(k == 0, 1.0, k) / COUNT
    first = np.where(k == 0, 0.0, math.pi / COUNT * sign / np.tan(angle))
    second = np.where(
        k == 0,
        -math.pi**2 / 3 - (2 * math.pi / COUNT) ** 2 / 6,
        -sign * (2 * math.pi**2 / COUNT**2) / np.sin(angle) ** 2,
    )
    return first, second


def halves(table):
    high = table.astype(ml_dtypes.bfloat16)
    low = (table - high.astype(np.float64)).astype(ml_dtypes.bfloat16)
    return np.stack([high, low])


def tables():
    def folded(size, value):
        gap = np.arange(size)[:, None] - np.arange(size)[None, :]
        return halves(np.concatenate([value(d, gap) for d in kernels()]))

    def plus(d, gap):
        return (d[gap % COUNT] + d[(gap + HALF) % COUNT]) / 2

    parts = []
    for sign in (1, -1):
        high, low = folded(
            QUARTER, lambda d, gap: (plus(d, gap) + sign * plus(d, gap + QUARTER)) / 2
        )
        parts.append(np.concatenate([high, low], axis=1))
    parts.extend(folded(HALF, lambda d, gap: (d[gap % COUNT] - d[(gap + HALF) % COUNT]) / 2))
    cell = np.arange(LANES)
    blocks = [
        np.concatenate(
            [d[(cell[None, :] - cell[:, None] - LANES * r) % COUNT] for d in kernels()], axis=1
        )
        for r in range(4)
    ]
    parts.extend(halves(np.concatenate(blocks)))
    return np.concatenate(parts)


def split(value):
    high = value.astype(BF16)
    return high, (value - high.astype(F32)).astype(BF16)


def three(left_high, left_low, right_high, right_low):
    total = jnp.dot(left_high, right_high, preferred_element_type=F32)
    total = total + jnp.dot(left_high, right_low, preferred_element_type=F32)
    return total + jnp.dot(left_low, right_high, preferred_element_type=F32)


def low_lanes(shape):
    return lax.broadcasted_iota(jnp.int32, shape, len(shape) - 1) < 64


def pack_kernel(x_hbm, msg_hbm, x_ref, msg_ref, in_sems, out_sems):
    gets = [
        pltpu.make_async_copy(x_hbm.at[:, 8 * g : 8 * g + 8], x_ref.at[g], in_sems.at[g])
        for g in range(4)
    ]
    puts = [
        pltpu.make_async_copy(msg_ref.at[g], msg_hbm.at[576 * g : 576 * g + 576], out_sems.at[g])
        for g in range(4)
    ]
    near = low_lanes((8, 128))
    for get in gets:
        get.start()
    for g in range(4):
        gets[g].wait()
        for i in range(ROWS):
            for low in range(2):
                at = pl.ds(36 * low + i, 8, stride=72)
                msg_ref[g, at, :] = x_ref[g, i, :, 128 * low : 128 * low + 128]
        for i in range(12):
            top, bottom = x_ref[g, i, :, 256:384], x_ref[g, i + 12, :, 256:384]
            lower = jnp.where(near, top, pltpu.roll(bottom, 64, 1))
            upper = jnp.where(near, pltpu.roll(top, 64, 1), bottom)
            msg_ref[g, pl.ds(24 + i, 8, stride=72), :] = lower
            msg_ref[g, pl.ds(60 + i, 8, stride=72), :] = upper
        puts[g].start()
    for put in puts:
        put.wait()


def pack(block):
    return pl.pallas_call(
        pack_kernel,
        in_specs=[pl.BlockSpec(memory_space=pltpu.HBM)],
        out_specs=pl.BlockSpec(memory_space=pltpu.HBM),
        out_shape=jax.ShapeDtypeStruct((2304, 128), F32),
        scratch_shapes=[
            pltpu.VMEM((4, ROWS, 8, LANES), F32),
            pltpu.VMEM((4, 576, 128), F32),
            pltpu.SemaphoreType.DMA((4,)),
            pltpu.SemaphoreType.DMA((4,)),
        ],
        compiler_params=pltpu.CompilerParams(vmem_limit_bytes=56 * 2**20),
    )(block)


def unpack_kernel(msg_ref, first_ref, second_ref):
    near = low_lanes((8, 128))
    for out_ref, full, part in ((first_ref, 0, 24), (second_ref, 48, 36)):
        for i in range(ROWS):
            for low in range(2):
                at = pl.ds(72 * low + full + i, 8, stride=144)
                out_ref[i, :, 128 * low : 128 * low + 128] = msg_ref[at, :]
        for i in range(12):
            lower = msg_ref[pl.ds(part + i, 8, stride=144), :]
            upper = msg_ref[pl.ds(72 + part + i, 8, stride=144), :]
            out_ref[i, :, 256:384] = jnp.where(near, lower, pltpu.roll(upper, 64, 1))
            out_ref[i + 12, :, 256:384] = jnp.where(near, pltpu.roll(lower, 64, 1), upper)


def unpack(message):
    out = jax.ShapeDtypeStruct((ROWS, PLANES, LANES), F32)
    return pl.pallas_call(
        unpack_kernel,
        grid=(4,),
        in_specs=[pl.BlockSpec((1152, 128), lambda i: (i, 0))],
        out_specs=[pl.BlockSpec((ROWS, 8, LANES), lambda i: (0, i, 0))] * 2,
        out_shape=(out, out),
        compiler_params=pltpu.CompilerParams(vmem_limit_bytes=16 * 2**20),
    )(message)


def cross_kernel(
    table_hbm, msg, out_hbm, small, large, out, line, got_small, got_large, table_sems, out_sems
):
    loads = [
        pltpu.make_async_copy(table_hbm.at[0:768], small.at[0], table_sems.at[0]),
        pltpu.make_async_copy(table_hbm.at[768:1536], small.at[1], table_sems.at[1]),
        pltpu.make_async_copy(table_hbm.at[1536:3072], large.at[0], table_sems.at[2]),
        pltpu.make_async_copy(table_hbm.at[3072:4608], large.at[1], table_sems.at[3]),
    ]
    puts = [pltpu.make_async_copy(out.at[z], out_hbm.at[z], out_sems.at[z]) for z in range(8)]
    for load in loads:
        load.start()

    for c in range(4):
        for y in range(4):
            at = 48 * (4 * c + y)
            top, bottom = msg[0, c, y], msg[1, c, y]
            for k, value in enumerate((top + bottom, top - bottom)):
                line[k, at : at + 24, 0:128] = value[0:24]
                line[k, at + 24 : at + 48, 0:128] = value[36:60]
                even, odd = value[24:36], value[60:72]
                parts = [even, pltpu.roll(even, 64, 1), odd, pltpu.roll(odd, 64, 1)]
                line[k, at : at + 48, 128:256] = jnp.concatenate(parts, axis=0)

    head, tail = line[0, :QUARTER, :], line[0, QUARTER:, :]
    for k, value in enumerate((head + tail, head - tail)):
        high, low = split(value)
        loads[k].wait()
        got_small[k] = three(small[k, :, :QUARTER], small[k, :, QUARTER:], high, low)
    high, low = split(line[1])
    loads[2].wait()
    total = jnp.dot(large[0], high, preferred_element_type=F32)
    total = total + jnp.dot(large[0], low, preferred_element_type=F32)
    loads[3].wait()
    got_large[...] = total + jnp.dot(large[1], high, preferred_element_type=F32)

    near = low_lanes((12, 128))
    for c in range(4):
        for y in range(4):
            for low in range(2):
                at = 48 * (4 * c + y) + ROWS * low
                for d, (full, part) in enumerate(((0, 24), (48, 36))):
                    minus = got_large[HALF * d + at : HALF * d + at + ROWS, :]
                    place = QUARTER * d + at % QUARTER
                    one = got_small[0, place : place + ROWS, :]
                    two = got_small[1, place : place + ROWS, :]
                    plus = one + two if at < QUARTER else one - two
                    for z, value in ((c, plus + minus), (c + 4, plus - minus)):
                        out[z, y, low, full : full + 24] = value[:, 0:128]
                        top, bottom = value[:12, 128:256], value[12:, 128:256]
                        out[z, y, low, part : part + 12] = jnp.where(
                            near, top, pltpu.roll(bottom, 64, 1)
                        )
        puts[c].start()
        puts[c + 4].start()
    for put in puts:
        put.wait()


def cross(table, message):
    return pl.pallas_call(
        cross_kernel,
        out_shape=jax.ShapeDtypeStruct((8, 4, 2, 72, 128), F32),
        in_specs=[pl.BlockSpec(memory_space=pltpu.HBM), pl.BlockSpec(memory_space=pltpu.VMEM)],
        out_specs=pl.BlockSpec(memory_space=pltpu.HBM),
        scratch_shapes=[
            pltpu.VMEM((2, HALF, HALF), BF16),
            pltpu.VMEM((2, COUNT, HALF), BF16),
            pltpu.VMEM((8, 4, 2, 72, 128), F32),
            pltpu.VMEM((2, HALF, 256), F32),
            pltpu.VMEM((2, HALF, 256), F32),
            pltpu.VMEM((COUNT, 256), F32),
            pltpu.SemaphoreType.DMA((4,)),
            pltpu.SemaphoreType.DMA((8,)),
        ],
        compiler_params=pltpu.CompilerParams(vmem_limit_bytes=50 * 2**20),
        cost_estimate=pl.CostEstimate(
            flops=3 * 2 * 3 * HALF * HALF * 256, bytes_accessed=12 * 2**20, transcendentals=0
        ),
    )(table, message.reshape(2, 4, 4, 72, 128))


def along_kernel(
    core_ref,
    table_hbm,
    own,
    near,
    far_a,
    far_b,
    far_near_a,
    far_near_b,
    first_ref,
    second_ref,
    table_ref,
    sem,
):
    core = core_ref[0]

    @pl.when(pl.program_id(0) == 0)
    def _():
        load = pltpu.make_async_copy(table_hbm.at[4608:7680], table_ref, sem)
        load.start()
        load.wait()

    def block_of(h, r):
        return table_ref[pl.ds(pl.multiple_of(COUNT * h + LANES * r, LANES), LANES), :]

    early = pl.program_id(0) == 0
    far = jnp.where(early, far_a[...], far_b[...])
    far_near = jnp.where(early, far_near_a[...], far_near_b[...])
    total = jnp.zeros((256, 2 * LANES), F32)
    pairs = ((own[...], 0), (near[...], 1 + 2 * core), (far, 2), (far_near, 3 - 2 * core))
    for block, r in pairs:
        high, low = split(block)
        total = total + three(high, low, block_of(0, r), block_of(1, r))
    first_ref[...] = total[:, :LANES]
    second_ref[...] = total[:, LANES:]


def along(core, table, *blocks):
    out = jax.ShapeDtypeStruct((ROWS * PLANES, LANES), F32)
    lines = pl.BlockSpec((256, LANES), lambda i, core: (i, 0))
    early = pl.BlockSpec((256, LANES), lambda i, core: (0, 0))
    late = pl.BlockSpec((256, LANES), lambda i, core: (jnp.maximum(i, 1) - 1, 0))
    return pl.pallas_call(
        along_kernel,
        grid_spec=pltpu.PrefetchScalarGridSpec(
            num_scalar_prefetch=1,
            grid=(3,),
            in_specs=[pl.BlockSpec(memory_space=pltpu.HBM)]
            + [lines, lines, early, late, early, late],
            out_specs=[lines] * 2,
            scratch_shapes=[
                pltpu.VMEM((2 * COUNT, 2 * LANES), BF16),
                pltpu.SemaphoreType.DMA,
            ],
        ),
        out_shape=(out, out),
        compiler_params=pltpu.CompilerParams(vmem_limit_bytes=50 * 2**20),
        cost_estimate=pl.CostEstimate(
            flops=2 * 3 * 768 * COUNT * 768, bytes_accessed=16 * 2**20, transcendentals=0
        ),
    )(core, table, *blocks)


def solution(mesh):
    fine = Mesh(mesh.devices.reshape(8, 4, 2, 2, 2), ("z", "y", "xl", "xh", "c"))
    table_t = tables()
    pair = [(0, 1), (1, 0)]

    def swap(message):
        return lax.all_to_all(message, ("z", "y", "xl"), split_axis=0, concat_axis=0, tiled=True)

    def shards(moments):
        grid = moments.shape
        table = jnp.asarray(table_t)
        own = moments.reshape(ROWS * PLANES, LANES)
        far_a = lax.ppermute(own[:256], "xh", pair)
        near = lax.ppermute(own, "c", pair)
        home = swap(pack(moments.reshape(ROWS, PLANES, LANES)).reshape(64, 9, 4, 128))
        home, far_a, near = lax.optimization_barrier((home, far_a, near))
        far_b = lax.ppermute(own[256:], "xh", pair)
        back = swap(cross(table, home).reshape(64, 72, 128))
        far_near_a = lax.ppermute(far_a, "c", pair)
        far_near_b = lax.ppermute(far_b, "c", pair)
        core = lax.axis_index("c").reshape(1)
        first_z, second_z = along(
            core, table, own, near, far_a, far_b, far_near_a, far_near_b
        )
        first_z, second_z, back = lax.optimization_barrier((first_z, second_z, back))
        first, second = unpack(back.reshape(4608, 128))
        return (
            first.reshape(grid),
            second.reshape(grid),
            first_z.reshape(grid),
            second_z.reshape(grid),
        )

    spec = P(("z", "y", "xl"), None, None, ("xh", "c"))
    return jax.shard_map(
        shards, mesh=fine, in_specs=(spec,), out_specs=(spec,) * 4, check_vma=False
    )
```

```python
import math

import jax
import jax.numpy as jnp
import ml_dtypes
import numpy as np
from jax import lax
from jax.experimental import pallas as pl
from jax.experimental.pallas import tpu as pltpu
from jax.sharding import Mesh
from jax.sharding import PartitionSpec as P

COUNT = 1536
HALF = COUNT // 2
QUARTER = COUNT // 4
ROWS = 24
LANES = 384
PLANES = 32
F32 = jnp.float32
BF16 = jnp.bfloat16


def kernels():
    k = np.arange(COUNT, dtype=np.float64)
    sign = np.where(np.arange(COUNT) % 2 == 0, 1.0, -1.0)
    angle = math.pi * np.where(k == 0, 1.0, k) / COUNT
    first = np.where(k == 0, 0.0, math.pi / COUNT * sign / np.tan(angle))
    second = np.where(
        k == 0,
        -math.pi**2 / 3 - (2 * math.pi / COUNT) ** 2 / 6,
        -sign * (2 * math.pi**2 / COUNT**2) / np.sin(angle) ** 2,
    )
    return first, second


def halves(table):
    high = table.astype(ml_dtypes.bfloat16)
    low = (table - high.astype(np.float64)).astype(ml_dtypes.bfloat16)
    return np.stack([high, low])


def cross_strips():
    def strip(block, value):
        gap = 2 * block + np.arange(block)[:, None] - np.arange(5 * block)[None, :]
        return halves(np.stack([value(d, gap) for d in kernels()]))

    def plus(d, gap):
        return (d[gap % COUNT] + d[(gap + HALF) % COUNT]) / 2

    both = strip(128, lambda d, gap: (plus(d, gap) + plus(d, gap + QUARTER)) / 2)
    cross = strip(128, lambda d, gap: (plus(d, gap) - plus(d, gap + QUARTER)) / 2)
    minus = strip(256, lambda d, gap: (d[gap % COUNT] - d[(gap + HALF) % COUNT]) / 2)
    return np.stack([both, cross]), minus


def along_table():
    cell = np.arange(LANES)
    blocks = [
        np.concatenate(
            [d[(cell[None, :] - cell[:, None] - LANES * r) % COUNT] for d in kernels()], axis=1
        )
        for r in range(4)
    ]
    return halves(np.stack(blocks))


def split(value):
    high = value.astype(BF16)
    return high, (value - high.astype(F32)).astype(BF16)


def three(left_high, left_low, right_high, right_low):
    total = jnp.dot(left_high, right_high, preferred_element_type=F32)
    total = total + jnp.dot(left_high, right_low, preferred_element_type=F32)
    return total + jnp.dot(left_low, right_high, preferred_element_type=F32)


def low_lanes(shape):
    return lax.broadcasted_iota(jnp.int32, shape, len(shape) - 1) < 64


def pack_kernel(x_hbm, msg_hbm, x_ref, msg_ref, in_sems, out_sems):
    gets = [
        pltpu.make_async_copy(x_hbm.at[:, 8 * g : 8 * g + 8], x_ref.at[g], in_sems.at[g])
        for g in range(4)
    ]
    puts = [
        pltpu.make_async_copy(msg_ref.at[g], msg_hbm.at[576 * g : 576 * g + 576], out_sems.at[g])
        for g in range(4)
    ]
    near = low_lanes((8, 128))
    for get in gets:
        get.start()
    for g in range(4):
        gets[g].wait()
        for i in range(ROWS):
            for low in range(2):
                at = pl.ds(36 * low + i, 8, stride=72)
                msg_ref[g, at, :] = x_ref[g, i, :, 128 * low : 128 * low + 128]
        for i in range(12):
            top, bottom = x_ref[g, i, :, 256:384], x_ref[g, i + 12, :, 256:384]
            lower = jnp.where(near, top, pltpu.roll(bottom, 64, 1))
            upper = jnp.where(near, pltpu.roll(top, 64, 1), bottom)
            msg_ref[g, pl.ds(24 + i, 8, stride=72), :] = lower
            msg_ref[g, pl.ds(60 + i, 8, stride=72), :] = upper
        puts[g].start()
    for put in puts:
        put.wait()


def pack(block):
    return pl.pallas_call(
        pack_kernel,
        in_specs=[pl.BlockSpec(memory_space=pltpu.HBM)],
        out_specs=pl.BlockSpec(memory_space=pltpu.HBM),
        out_shape=jax.ShapeDtypeStruct((2304, 128), F32),
        scratch_shapes=[
            pltpu.VMEM((4, ROWS, 8, LANES), F32),
            pltpu.VMEM((4, 576, 128), F32),
            pltpu.SemaphoreType.DMA((4,)),
            pltpu.SemaphoreType.DMA((4,)),
        ],
        compiler_params=pltpu.CompilerParams(vmem_limit_bytes=56 * 2**20),
    )(block)


def unpack_kernel(msg_ref, first_ref, second_ref):
    near = low_lanes((8, 128))
    for out_ref, full, part in ((first_ref, 0, 24), (second_ref, 48, 36)):
        for i in range(ROWS):
            for low in range(2):
                at = pl.ds(72 * low + full + i, 8, stride=144)
                out_ref[i, :, 128 * low : 128 * low + 128] = msg_ref[at, :]
        for i in range(12):
            lower = msg_ref[pl.ds(part + i, 8, stride=144), :]
            upper = msg_ref[pl.ds(72 + part + i, 8, stride=144), :]
            out_ref[i, :, 256:384] = jnp.where(near, lower, pltpu.roll(upper, 64, 1))
            out_ref[i + 12, :, 256:384] = jnp.where(near, pltpu.roll(lower, 64, 1), upper)


def unpack(message):
    out = jax.ShapeDtypeStruct((ROWS, PLANES, LANES), F32)
    return pl.pallas_call(
        unpack_kernel,
        grid=(4,),
        in_specs=[pl.BlockSpec((1152, 128), lambda i: (i, 0))],
        out_specs=[pl.BlockSpec((ROWS, 8, LANES), lambda i: (0, i, 0))] * 2,
        out_shape=(out, out),
        compiler_params=pltpu.CompilerParams(vmem_limit_bytes=16 * 2**20),
    )(message)


def cross_kernel(
    small_hbm,
    large_hbm,
    msg_hbm,
    out_hbm,
    small_strip,
    large_strip,
    small,
    large,
    msg,
    out,
    line,
    got_small,
    got_large,
    in_sems,
    table_sems,
    out_sems,
):
    gets = [
        pltpu.make_async_copy(msg_hbm.at[:, c], msg.at[c], in_sems.at[c]) for c in range(4)
    ]
    strips = [
        pltpu.make_async_copy(small_hbm, small_strip, table_sems.at[0]),
        pltpu.make_async_copy(large_hbm, large_strip, table_sems.at[1]),
    ]
    puts = [pltpu.make_async_copy(out.at[z], out_hbm.at[z], out_sems.at[z]) for z in range(8)]
    for copy in gets + strips:
        copy.start()

    for c in range(4):
        gets[c].wait()
        for y in range(4):
            at = 48 * (4 * c + y)
            top, bottom = msg[c, 0, y], msg[c, 1, y]
            for k, value in enumerate((top + bottom, top - bottom)):
                line[k, at : at + 24, 0:128] = value[0:24]
                line[k, at + 24 : at + 48, 0:128] = value[36:60]
                even, odd = value[24:36], value[60:72]
                parts = [even, pltpu.roll(even, 64, 1), odd, pltpu.roll(odd, 64, 1)]
                line[k, at : at + 48, 128:256] = jnp.concatenate(parts, axis=0)

    for copy in strips:
        copy.wait()
    for h in range(2):
        for d in range(2):
            for i in range(3):
                rows = slice(QUARTER * d + 128 * i, QUARTER * d + 128 * i + 128)
                lanes = slice(128 * (2 - i), 128 * (2 - i) + QUARTER)
                for k in range(2):
                    small[k, h, rows, :] = small_strip[k, h, d, :, lanes]
    for h in range(2):
        for d in range(2):
            for i in range(3):
                rows = slice(HALF * d + 256 * i, HALF * d + 256 * i + 256)
                lanes = slice(256 * (2 - i), 256 * (2 - i) + HALF)
                large[h, rows, :] = large_strip[h, d, :, lanes]

    head, tail = line[0, :QUARTER, :], line[0, QUARTER:, :]
    for k, value in enumerate((head + tail, head - tail)):
        high, low = split(value)
        got_small[k] = three(small[k, 0], small[k, 1], high, low)
    high, low = split(line[1])
    total = jnp.dot(large[0], high, preferred_element_type=F32)
    total = total + jnp.dot(large[0], low, preferred_element_type=F32)
    got_large[...] = total + jnp.dot(large[1], high, preferred_element_type=F32)

    near = low_lanes((12, 128))
    for c in range(4):
        for y in range(4):
            for low in range(2):
                at = 48 * (4 * c + y) + ROWS * low
                for d, (full, part) in enumerate(((0, 24), (48, 36))):
                    minus = got_large[HALF * d + at : HALF * d + at + ROWS, :]
                    place = QUARTER * d + at % QUARTER
                    one = got_small[0, place : place + ROWS, :]
                    two = got_small[1, place : place + ROWS, :]
                    plus = one + two if at < QUARTER else one - two
                    for z, value in ((c, plus + minus), (c + 4, plus - minus)):
                        out[z, y, low, full : full + 24] = value[:, 0:128]
                        top, bottom = value[:12, 128:256], value[12:, 128:256]
                        out[z, y, low, part : part + 12] = jnp.where(
                            near, top, pltpu.roll(bottom, 64, 1)
                        )
        puts[c].start()
        puts[c + 4].start()
    for put in puts:
        put.wait()


def cross(small, large, message):
    return pl.pallas_call(
        cross_kernel,
        out_shape=jax.ShapeDtypeStruct((8, 4, 2, 72, 128), F32),
        in_specs=[
            pl.BlockSpec(memory_space=pltpu.HBM),
            pl.BlockSpec(memory_space=pltpu.HBM),
            pl.BlockSpec(memory_space=pl.ANY),
        ],
        out_specs=pl.BlockSpec(memory_space=pltpu.HBM),
        scratch_shapes=[
            pltpu.VMEM(small.shape, BF16),
            pltpu.VMEM(large.shape, BF16),
            pltpu.VMEM((2, 2, HALF, QUARTER), BF16),
            pltpu.VMEM((2, COUNT, HALF), BF16),
            pltpu.VMEM((4, 2, 4, 72, 128), F32),
            pltpu.VMEM((8, 4, 2, 72, 128), F32),
            pltpu.VMEM((2, HALF, 256), F32),
            pltpu.VMEM((2, HALF, 256), F32),
            pltpu.VMEM((COUNT, 256), F32),
            pltpu.SemaphoreType.DMA((4,)),
            pltpu.SemaphoreType.DMA((2,)),
            pltpu.SemaphoreType.DMA((8,)),
        ],
        compiler_params=pltpu.CompilerParams(vmem_limit_bytes=60 * 2**20),
        cost_estimate=pl.CostEstimate(
            flops=3 * 2 * 3 * HALF * HALF * 256, bytes_accessed=12 * 2**20, transcendentals=0
        ),
    )(small, large, message.reshape(2, 4, 4, 72, 128))


def along_kernel(
    core_ref, table_ref, own, near, far_a, far_b, far_near_a, far_near_b, first_ref, second_ref
):
    core = core_ref[0]
    early = pl.program_id(0) == 0
    far = jnp.where(early, far_a[...], far_b[...])
    far_near = jnp.where(early, far_near_a[...], far_near_b[...])
    total = jnp.zeros((256, 2 * LANES), F32)
    pairs = ((own[...], 0), (near[...], 1 + 2 * core), (far, 2), (far_near, 3 - 2 * core))
    for block, r in pairs:
        high, low = split(block)
        total = total + three(high, low, table_ref[0, r], table_ref[1, r])
    first_ref[...] = total[:, :LANES]
    second_ref[...] = total[:, LANES:]


def along(core, table, *blocks):
    out = jax.ShapeDtypeStruct((ROWS * PLANES, LANES), F32)
    lines = pl.BlockSpec((256, LANES), lambda i, core: (i, 0))
    early = pl.BlockSpec((256, LANES), lambda i, core: (0, 0))
    late = pl.BlockSpec((256, LANES), lambda i, core: (jnp.maximum(i, 1) - 1, 0))
    return pl.pallas_call(
        along_kernel,
        grid_spec=pltpu.PrefetchScalarGridSpec(
            num_scalar_prefetch=1,
            grid=(3,),
            in_specs=[pl.BlockSpec((2, 4, LANES, 2 * LANES), lambda i, core: (0, 0, 0, 0))]
            + [lines, lines, early, late, early, late],
            out_specs=[lines] * 2,
        ),
        out_shape=(out, out),
        compiler_params=pltpu.CompilerParams(vmem_limit_bytes=24 * 2**20),
        cost_estimate=pl.CostEstimate(
            flops=2 * 3 * 768 * COUNT * 768, bytes_accessed=16 * 2**20, transcendentals=0
        ),
    )(core, table, *blocks)


def solution(mesh):
    fine = Mesh(mesh.devices.reshape(8, 4, 2, 2, 2), ("z", "y", "xl", "xh", "c"))
    small_t, large_t = cross_strips()
    along_t = along_table()
    pair = [(0, 1), (1, 0)]

    def swap(message):
        return lax.all_to_all(message, ("z", "y", "xl"), split_axis=0, concat_axis=0, tiled=True)

    def shards(moments):
        grid = moments.shape
        own = moments.reshape(ROWS * PLANES, LANES)
        far_a = lax.ppermute(own[:256], "xh", pair)
        near = lax.ppermute(own, "c", pair)
        home = swap(pack(moments.reshape(ROWS, PLANES, LANES)).reshape(64, 9, 4, 128))
        home, far_a, near = lax.optimization_barrier((home, far_a, near))
        far_b = lax.ppermute(own[256:], "xh", pair)
        back = swap(cross(jnp.asarray(small_t), jnp.asarray(large_t), home).reshape(64, 72, 128))
        far_near_a = lax.ppermute(far_a, "c", pair)
        far_near_b = lax.ppermute(far_b, "c", pair)
        core = lax.axis_index("c").reshape(1)
        first_z, second_z = along(
            core, jnp.asarray(along_t), own, near, far_a, far_b, far_near_a, far_near_b
        )
        first_z, second_z, back = lax.optimization_barrier((first_z, second_z, back))
        first, second = unpack(back.reshape(4608, 128))
        return (
            first.reshape(grid),
            second.reshape(grid),
            first_z.reshape(grid),
            second_z.reshape(grid),
        )

    spec = P(("z", "y", "xl"), None, None, ("xh", "c"))
    return jax.shard_map(
        shards, mesh=fine, in_specs=(spec,), out_specs=(spec,) * 4, check_vma=False
    )
```

```python
import math

import jax
import jax.numpy as jnp
import ml_dtypes
import numpy as np
from jax import lax
from jax.experimental import pallas as pl
from jax.experimental.pallas import tpu as pltpu
from jax.sharding import Mesh
from jax.sharding import PartitionSpec as P

COUNT = 1536
HALF = COUNT // 2
QUARTER = COUNT // 4
ROWS = 24
LANES = 384
PLANES = 32
F32 = jnp.float32
BF16 = jnp.bfloat16


def kernels():
    k = np.arange(COUNT, dtype=np.float64)
    sign = np.where(np.arange(COUNT) % 2 == 0, 1.0, -1.0)
    angle = math.pi * np.where(k == 0, 1.0, k) / COUNT
    first = np.where(k == 0, 0.0, math.pi / COUNT * sign / np.tan(angle))
    second = np.where(
        k == 0,
        -math.pi**2 / 3 - (2 * math.pi / COUNT) ** 2 / 6,
        -sign * (2 * math.pi**2 / COUNT**2) / np.sin(angle) ** 2,
    )
    return first, second


def halves(table):
    high = table.astype(ml_dtypes.bfloat16)
    low = (table - high.astype(np.float64)).astype(ml_dtypes.bfloat16)
    return np.stack([high, low])


def cross_strips():
    def strip(block, value):
        gap = 2 * block + np.arange(block)[:, None] - np.arange(5 * block)[None, :]
        return halves(np.stack([value(d, gap) for d in kernels()]))

    def plus(d, gap):
        return (d[gap % COUNT] + d[(gap + HALF) % COUNT]) / 2

    both = strip(128, lambda d, gap: (plus(d, gap) + plus(d, gap + QUARTER)) / 2)
    cross = strip(128, lambda d, gap: (plus(d, gap) - plus(d, gap + QUARTER)) / 2)
    minus = strip(256, lambda d, gap: (d[gap % COUNT] - d[(gap + HALF) % COUNT]) / 2)
    return np.stack([both, cross]), minus


def along_table():
    cell = np.arange(LANES)
    blocks = [
        np.concatenate(
            [d[(cell[None, :] - cell[:, None] - LANES * r) % COUNT] for d in kernels()], axis=1
        )
        for r in range(4)
    ]
    return halves(np.stack(blocks))


def split(value):
    high = value.astype(BF16)
    return high, (value - high.astype(F32)).astype(BF16)


def three(left_high, left_low, right_high, right_low):
    total = jnp.dot(left_high, right_high, preferred_element_type=F32)
    total = total + jnp.dot(left_high, right_low, preferred_element_type=F32)
    return total + jnp.dot(left_low, right_high, preferred_element_type=F32)


def low_lanes(shape):
    return lax.broadcasted_iota(jnp.int32, shape, len(shape) - 1) < 64


def pack_kernel(x_hbm, msg_ref, x_ref, sems):
    gets = [
        pltpu.make_async_copy(x_hbm.at[:, 8 * g : 8 * g + 8], x_ref.at[g], sems.at[g])
        for g in range(4)
    ]
    near = low_lanes((8, 128))
    for get in gets:
        get.start()
    for g in range(4):
        base = 576 * g
        gets[g].wait()
        for i in range(ROWS):
            for low in range(2):
                at = pl.ds(base + 36 * low + i, 8, stride=72)
                msg_ref[at, :] = x_ref[g, i, :, 128 * low : 128 * low + 128]
        for i in range(12):
            top, bottom = x_ref[g, i, :, 256:384], x_ref[g, i + 12, :, 256:384]
            lower = jnp.where(near, top, pltpu.roll(bottom, 64, 1))
            upper = jnp.where(near, pltpu.roll(top, 64, 1), bottom)
            msg_ref[pl.ds(base + 24 + i, 8, stride=72), :] = lower
            msg_ref[pl.ds(base + 60 + i, 8, stride=72), :] = upper


def pack(block):
    return pl.pallas_call(
        pack_kernel,
        in_specs=[pl.BlockSpec(memory_space=pltpu.HBM)],
        out_specs=pl.BlockSpec(memory_space=pltpu.VMEM),
        out_shape=jax.ShapeDtypeStruct((2304, 128), F32),
        scratch_shapes=[
            pltpu.VMEM((4, ROWS, 8, LANES), F32),
            pltpu.SemaphoreType.DMA((4,)),
        ],
        compiler_params=pltpu.CompilerParams(vmem_limit_bytes=56 * 2**20),
    )(block)


def unpack_kernel(msg_ref, first_hbm, second_hbm, out_ref, sems):
    near = low_lanes((8, 128))
    puts = []
    for g in range(4):
        base = 1152 * g
        for d, (out_hbm, full, part) in enumerate(((first_hbm, 0, 24), (second_hbm, 48, 36))):
            for i in range(ROWS):
                for low in range(2):
                    at = pl.ds(base + 72 * low + full + i, 8, stride=144)
                    out_ref[d, g, i, :, 128 * low : 128 * low + 128] = msg_ref[at, :]
            for i in range(12):
                lower = msg_ref[pl.ds(base + part + i, 8, stride=144), :]
                upper = msg_ref[pl.ds(base + 72 + part + i, 8, stride=144), :]
                out_ref[d, g, i, :, 256:384] = jnp.where(near, lower, pltpu.roll(upper, 64, 1))
                out_ref[d, g, i + 12, :, 256:384] = jnp.where(
                    near, pltpu.roll(lower, 64, 1), upper
                )
            put = pltpu.make_async_copy(
                out_ref.at[d, g], out_hbm.at[:, 8 * g : 8 * g + 8], sems.at[2 * g + d]
            )
            put.start()
            puts.append(put)
    for put in puts:
        put.wait()


def unpack(message):
    out = jax.ShapeDtypeStruct((ROWS, PLANES, LANES), F32)
    return pl.pallas_call(
        unpack_kernel,
        in_specs=[pl.BlockSpec(memory_space=pltpu.VMEM)],
        out_specs=[pl.BlockSpec(memory_space=pltpu.HBM)] * 2,
        out_shape=(out, out),
        scratch_shapes=[
            pltpu.VMEM((2, 4, ROWS, 8, LANES), F32),
            pltpu.SemaphoreType.DMA((8,)),
        ],
        compiler_params=pltpu.CompilerParams(vmem_limit_bytes=16 * 2**20),
    )(message)


def cross_kernel(
    small_hbm,
    large_hbm,
    msg_hbm,
    out_hbm,
    small_strip,
    large_strip,
    small,
    large,
    msg,
    out,
    line,
    got_small,
    got_large,
    in_sems,
    table_sems,
    out_sems,
):
    gets = [
        pltpu.make_async_copy(msg_hbm.at[:, c], msg.at[c], in_sems.at[c]) for c in range(4)
    ]
    strips = [
        pltpu.make_async_copy(small_hbm, small_strip, table_sems.at[0]),
        pltpu.make_async_copy(large_hbm, large_strip, table_sems.at[1]),
    ]
    puts = [pltpu.make_async_copy(out.at[z], out_hbm.at[z], out_sems.at[z]) for z in range(8)]
    for copy in gets + strips:
        copy.start()

    for c in range(4):
        gets[c].wait()
        for y in range(4):
            at = 48 * (4 * c + y)
            top, bottom = msg[c, 0, y], msg[c, 1, y]
            for k, value in enumerate((top + bottom, top - bottom)):
                line[k, at : at + 24, 0:128] = value[0:24]
                line[k, at + 24 : at + 48, 0:128] = value[36:60]
                even, odd = value[24:36], value[60:72]
                parts = [even, pltpu.roll(even, 64, 1), odd, pltpu.roll(odd, 64, 1)]
                line[k, at : at + 48, 128:256] = jnp.concatenate(parts, axis=0)

    for copy in strips:
        copy.wait()
    for h in range(2):
        for d in range(2):
            for i in range(3):
                rows = slice(QUARTER * d + 128 * i, QUARTER * d + 128 * i + 128)
                lanes = slice(128 * (2 - i), 128 * (2 - i) + QUARTER)
                for k in range(2):
                    small[k, h, rows, :] = small_strip[k, h, d, :, lanes]
    for h in range(2):
        for d in range(2):
            for i in range(3):
                rows = slice(HALF * d + 256 * i, HALF * d + 256 * i + 256)
                lanes = slice(256 * (2 - i), 256 * (2 - i) + HALF)
                large[h, rows, :] = large_strip[h, d, :, lanes]

    head, tail = line[0, :QUARTER, :], line[0, QUARTER:, :]
    for k, value in enumerate((head + tail, head - tail)):
        high, low = split(value)
        got_small[k] = three(small[k, 0], small[k, 1], high, low)
    high, low = split(line[1])
    total = jnp.dot(large[0], high, preferred_element_type=F32)
    total = total + jnp.dot(large[0], low, preferred_element_type=F32)
    got_large[...] = total + jnp.dot(large[1], high, preferred_element_type=F32)

    near = low_lanes((12, 128))
    for c in range(4):
        for y in range(4):
            for low in range(2):
                at = 48 * (4 * c + y) + ROWS * low
                for d, (full, part) in enumerate(((0, 24), (48, 36))):
                    minus = got_large[HALF * d + at : HALF * d + at + ROWS, :]
                    place = QUARTER * d + at % QUARTER
                    one = got_small[0, place : place + ROWS, :]
                    two = got_small[1, place : place + ROWS, :]
                    plus = one + two if at < QUARTER else one - two
                    for z, value in ((c, plus + minus), (c + 4, plus - minus)):
                        out[z, y, low, full : full + 24] = value[:, 0:128]
                        top, bottom = value[:12, 128:256], value[12:, 128:256]
                        out[z, y, low, part : part + 12] = jnp.where(
                            near, top, pltpu.roll(bottom, 64, 1)
                        )
        puts[c].start()
        puts[c + 4].start()
    for put in puts:
        put.wait()


def cross(small, large, message):
    return pl.pallas_call(
        cross_kernel,
        out_shape=jax.ShapeDtypeStruct((8, 4, 2, 72, 128), F32),
        in_specs=[
            pl.BlockSpec(memory_space=pltpu.HBM),
            pl.BlockSpec(memory_space=pltpu.HBM),
            pl.BlockSpec(memory_space=pl.ANY),
        ],
        out_specs=pl.BlockSpec(memory_space=pltpu.HBM),
        scratch_shapes=[
            pltpu.VMEM(small.shape, BF16),
            pltpu.VMEM(large.shape, BF16),
            pltpu.VMEM((2, 2, HALF, QUARTER), BF16),
            pltpu.VMEM((2, COUNT, HALF), BF16),
            pltpu.VMEM((4, 2, 4, 72, 128), F32),
            pltpu.VMEM((8, 4, 2, 72, 128), F32),
            pltpu.VMEM((2, HALF, 256), F32),
            pltpu.VMEM((2, HALF, 256), F32),
            pltpu.VMEM((COUNT, 256), F32),
            pltpu.SemaphoreType.DMA((4,)),
            pltpu.SemaphoreType.DMA((2,)),
            pltpu.SemaphoreType.DMA((8,)),
        ],
        compiler_params=pltpu.CompilerParams(vmem_limit_bytes=60 * 2**20),
        cost_estimate=pl.CostEstimate(
            flops=3 * 2 * 3 * HALF * HALF * 256, bytes_accessed=12 * 2**20, transcendentals=0
        ),
    )(small, large, message.reshape(2, 4, 4, 72, 128))


def along_kernel(
    core_ref, table_ref, own, near, far_a, far_b, far_near_a, far_near_b, first_ref, second_ref
):
    core = core_ref[0]
    early = pl.program_id(0) == 0
    far = jnp.where(early, far_a[...], far_b[...])
    far_near = jnp.where(early, far_near_a[...], far_near_b[...])
    total = jnp.zeros((256, 2 * LANES), F32)
    pairs = ((own[...], 0), (near[...], 1 + 2 * core), (far, 2), (far_near, 3 - 2 * core))
    for block, r in pairs:
        high, low = split(block)
        total = total + three(high, low, table_ref[0, r], table_ref[1, r])
    first_ref[...] = total[:, :LANES]
    second_ref[...] = total[:, LANES:]


def along(core, table, *blocks):
    out = jax.ShapeDtypeStruct((ROWS * PLANES, LANES), F32)
    lines = pl.BlockSpec((256, LANES), lambda i, core: (i, 0))
    early = pl.BlockSpec((256, LANES), lambda i, core: (0, 0))
    late = pl.BlockSpec((256, LANES), lambda i, core: (jnp.maximum(i, 1) - 1, 0))
    return pl.pallas_call(
        along_kernel,
        grid_spec=pltpu.PrefetchScalarGridSpec(
            num_scalar_prefetch=1,
            grid=(3,),
            in_specs=[pl.BlockSpec((2, 4, LANES, 2 * LANES), lambda i, core: (0, 0, 0, 0))]
            + [lines, lines, early, late, early, late],
            out_specs=[lines] * 2,
        ),
        out_shape=(out, out),
        compiler_params=pltpu.CompilerParams(vmem_limit_bytes=24 * 2**20),
        cost_estimate=pl.CostEstimate(
            flops=2 * 3 * 768 * COUNT * 768, bytes_accessed=16 * 2**20, transcendentals=0
        ),
    )(core, table, *blocks)


def solution(mesh):
    fine = Mesh(mesh.devices.reshape(8, 4, 2, 2, 2), ("z", "y", "xl", "xh", "c"))
    small_t, large_t = cross_strips()
    along_t = along_table()
    pair = [(0, 1), (1, 0)]

    def swap(message):
        return lax.all_to_all(message, ("z", "y", "xl"), split_axis=0, concat_axis=0, tiled=True)

    def shards(moments):
        grid = moments.shape
        own = moments.reshape(ROWS * PLANES, LANES)
        far_a = lax.ppermute(own[:256], "xh", pair)
        near = lax.ppermute(own, "c", pair)
        home = swap(pack(moments.reshape(ROWS, PLANES, LANES)).reshape(64, 9, 4, 128))
        home, far_a, near = lax.optimization_barrier((home, far_a, near))
        far_b = lax.ppermute(own[256:], "xh", pair)
        back = swap(cross(jnp.asarray(small_t), jnp.asarray(large_t), home).reshape(64, 72, 128))
        far_near_a = lax.ppermute(far_a, "c", pair)
        far_near_b = lax.ppermute(far_b, "c", pair)
        core = lax.axis_index("c").reshape(1)
        first_z, second_z = along(
            core, jnp.asarray(along_t), own, near, far_a, far_b, far_near_a, far_near_b
        )
        first_z, second_z, back = lax.optimization_barrier((first_z, second_z, back))
        first, second = unpack(back.reshape(4608, 128))
        return (
            first.reshape(grid),
            second.reshape(grid),
            first_z.reshape(grid),
            second_z.reshape(grid),
        )

    spec = P(("z", "y", "xl"), None, None, ("xh", "c"))
    return jax.shard_map(
        shards, mesh=fine, in_specs=(spec,), out_specs=(spec,) * 4, check_vma=False
    )
```

```python
import math

import jax
import jax.numpy as jnp
import ml_dtypes
import numpy as np
from jax import lax
from jax.experimental import pallas as pl
from jax.experimental.pallas import tpu as pltpu
from jax.sharding import Mesh
from jax.sharding import PartitionSpec as P

COUNT = 1536
HALF = COUNT // 2
QUARTER = COUNT // 4
ROWS = 24
LANES = 384
PLANES = 32
F32 = jnp.float32
BF16 = jnp.bfloat16


def kernels():
    k = np.arange(COUNT, dtype=np.float64)
    sign = np.where(np.arange(COUNT) % 2 == 0, 1.0, -1.0)
    angle = math.pi * np.where(k == 0, 1.0, k) / COUNT
    first = np.where(k == 0, 0.0, math.pi / COUNT * sign / np.tan(angle))
    second = np.where(
        k == 0,
        -math.pi**2 / 3 - (2 * math.pi / COUNT) ** 2 / 6,
        -sign * (2 * math.pi**2 / COUNT**2) / np.sin(angle) ** 2,
    )
    return first, second


def halves(table):
    high = table.astype(ml_dtypes.bfloat16)
    low = (table - high.astype(np.float64)).astype(ml_dtypes.bfloat16)
    return np.stack([high, low])


def cross_strips():
    def strip(block, value):
        gap = 2 * block + np.arange(block)[:, None] - np.arange(5 * block)[None, :]
        return halves(np.stack([value(d, gap) for d in kernels()]))

    def plus(d, gap):
        return (d[gap % COUNT] + d[(gap + HALF) % COUNT]) / 2

    both = strip(128, lambda d, gap: (plus(d, gap) + plus(d, gap + QUARTER)) / 2)
    cross = strip(128, lambda d, gap: (plus(d, gap) - plus(d, gap + QUARTER)) / 2)
    minus = strip(256, lambda d, gap: (d[gap % COUNT] - d[(gap + HALF) % COUNT]) / 2)
    return np.stack([both, cross]), minus


def along_table():
    cell = np.arange(LANES)
    blocks = [
        np.concatenate(
            [d[(cell[None, :] - cell[:, None] - LANES * r) % COUNT] for d in kernels()], axis=1
        )
        for r in range(4)
    ]
    return halves(np.stack(blocks))


def split(value):
    high = value.astype(BF16)
    return high, (value - high.astype(F32)).astype(BF16)


def three(left_high, left_low, right_high, right_low):
    total = jnp.dot(left_high, right_high, preferred_element_type=F32)
    total = total + jnp.dot(left_high, right_low, preferred_element_type=F32)
    return total + jnp.dot(left_low, right_high, preferred_element_type=F32)


def low_lanes(shape):
    return lax.broadcasted_iota(jnp.int32, shape, len(shape) - 1) < 64


def pack_kernel(x_hbm, msg_hbm, x_ref, msg_ref, in_sems, out_sems):
    gets = [
        pltpu.make_async_copy(x_hbm.at[:, 8 * g : 8 * g + 8], x_ref.at[g], in_sems.at[g])
        for g in range(4)
    ]
    puts = [
        pltpu.make_async_copy(msg_ref.at[g], msg_hbm.at[576 * g : 576 * g + 576], out_sems.at[g])
        for g in range(4)
    ]
    near = low_lanes((8, 128))
    for get in gets:
        get.start()
    for g in range(4):
        gets[g].wait()
        for i in range(ROWS):
            for low in range(2):
                at = pl.ds(36 * low + i, 8, stride=72)
                msg_ref[g, at, :] = x_ref[g, i, :, 128 * low : 128 * low + 128]
        for i in range(12):
            top, bottom = x_ref[g, i, :, 256:384], x_ref[g, i + 12, :, 256:384]
            lower = jnp.where(near, top, pltpu.roll(bottom, 64, 1))
            upper = jnp.where(near, pltpu.roll(top, 64, 1), bottom)
            msg_ref[g, pl.ds(24 + i, 8, stride=72), :] = lower
            msg_ref[g, pl.ds(60 + i, 8, stride=72), :] = upper
        puts[g].start()
    for put in puts:
        put.wait()


def pack(block):
    return pl.pallas_call(
        pack_kernel,
        in_specs=[pl.BlockSpec(memory_space=pltpu.HBM)],
        out_specs=pl.BlockSpec(memory_space=pltpu.HBM),
        out_shape=jax.ShapeDtypeStruct((2304, 128), F32),
        scratch_shapes=[
            pltpu.VMEM((4, ROWS, 8, LANES), F32),
            pltpu.VMEM((4, 576, 128), F32),
            pltpu.SemaphoreType.DMA((4,)),
            pltpu.SemaphoreType.DMA((4,)),
        ],
        compiler_params=pltpu.CompilerParams(vmem_limit_bytes=56 * 2**20),
    )(block)


def unpack_kernel(msg_ref, first_hbm, second_hbm, out_ref, sems):
    near = low_lanes((8, 128))
    puts = []
    for g in range(4):
        base = 1152 * g
        for d, (out_hbm, full, part) in enumerate(((first_hbm, 0, 24), (second_hbm, 48, 36))):
            for i in range(ROWS):
                for low in range(2):
                    at = pl.ds(base + 72 * low + full + i, 8, stride=144)
                    out_ref[d, g, i, :, 128 * low : 128 * low + 128] = msg_ref[at, :]
            for i in range(12):
                lower = msg_ref[pl.ds(base + part + i, 8, stride=144), :]
                upper = msg_ref[pl.ds(base + 72 + part + i, 8, stride=144), :]
                out_ref[d, g, i, :, 256:384] = jnp.where(near, lower, pltpu.roll(upper, 64, 1))
                out_ref[d, g, i + 12, :, 256:384] = jnp.where(
                    near, pltpu.roll(lower, 64, 1), upper
                )
            put = pltpu.make_async_copy(
                out_ref.at[d, g], out_hbm.at[:, 8 * g : 8 * g + 8], sems.at[2 * g + d]
            )
            put.start()
            puts.append(put)
    for put in puts:
        put.wait()


def unpack(message):
    out = jax.ShapeDtypeStruct((ROWS, PLANES, LANES), F32)
    return pl.pallas_call(
        unpack_kernel,
        in_specs=[pl.BlockSpec(memory_space=pltpu.VMEM)],
        out_specs=[pl.BlockSpec(memory_space=pltpu.HBM)] * 2,
        out_shape=(out, out),
        scratch_shapes=[
            pltpu.VMEM((2, 4, ROWS, 8, LANES), F32),
            pltpu.SemaphoreType.DMA((8,)),
        ],
        compiler_params=pltpu.CompilerParams(vmem_limit_bytes=16 * 2**20),
    )(message)


def cross_kernel(
    small_hbm,
    large_hbm,
    msg_hbm,
    out_hbm,
    small_strip,
    large_strip,
    small,
    msg,
    out,
    line,
    got_small,
    got_large,
    in_sems,
    table_sems,
    out_sems,
):
    gets = [
        pltpu.make_async_copy(msg_hbm.at[:, c], msg.at[c], in_sems.at[c]) for c in range(4)
    ]
    strips = [
        pltpu.make_async_copy(small_hbm, small_strip, table_sems.at[0]),
        pltpu.make_async_copy(large_hbm, large_strip, table_sems.at[1]),
    ]
    puts = [pltpu.make_async_copy(out.at[z], out_hbm.at[z], out_sems.at[z]) for z in range(8)]
    for copy in gets + strips:
        copy.start()

    for c in range(4):
        gets[c].wait()
        for y in range(4):
            at = 48 * (4 * c + y)
            top, bottom = msg[c, 0, y], msg[c, 1, y]
            for k, value in enumerate((top + bottom, top - bottom)):
                line[k, at : at + 24, 0:128] = value[0:24]
                line[k, at + 24 : at + 48, 0:128] = value[36:60]
                even, odd = value[24:36], value[60:72]
                parts = [even, pltpu.roll(even, 64, 1), odd, pltpu.roll(odd, 64, 1)]
                line[k, at : at + 48, 128:256] = jnp.concatenate(parts, axis=0)

    for copy in strips:
        copy.wait()
    for h in range(2):
        for d in range(2):
            for i in range(3):
                rows = slice(QUARTER * d + 128 * i, QUARTER * d + 128 * i + 128)
                lanes = slice(128 * (2 - i), 128 * (2 - i) + QUARTER)
                for k in range(2):
                    small[k, h, rows, :] = small_strip[k, h, d, :, lanes]
    head, tail = line[0, :QUARTER, :], line[0, QUARTER:, :]
    for k, value in enumerate((head + tail, head - tail)):
        high, low = split(value)
        got_small[k] = three(small[k, 0], small[k, 1], high, low)

    high, low = split(line[1])
    near = low_lanes((12, 128))

    def products(i):
        for d in range(2):
            lanes = slice(256 * (2 - i), 256 * (2 - i) + HALF)
            left = large_strip[0, d, :, lanes], large_strip[1, d, :, lanes]
            got_large[HALF * d + 256 * i : HALF * d + 256 * i + 256, :] = three(*left, high, low)

    def close(c):
        for y in range(4):
            for part_of in range(2):
                at = 48 * (4 * c + y) + ROWS * part_of
                for d, (full, part) in enumerate(((0, 24), (48, 36))):
                    minus = got_large[HALF * d + at : HALF * d + at + ROWS, :]
                    place = QUARTER * d + at % QUARTER
                    one = got_small[0, place : place + ROWS, :]
                    two = got_small[1, place : place + ROWS, :]
                    plus = one + two if at < QUARTER else one - two
                    for z, value in ((c, plus + minus), (c + 4, plus - minus)):
                        out[z, y, part_of, full : full + 24] = value[:, 0:128]
                        top, bottom = value[:12, 128:256], value[12:, 128:256]
                        out[z, y, part_of, part : part + 12] = jnp.where(
                            near, top, pltpu.roll(bottom, 64, 1)
                        )
        puts[c].start()
        puts[c + 4].start()

    products(0)
    products(1)
    close(0)
    products(2)
    close(1)
    close(2)
    close(3)
    for put in puts:
        put.wait()


def cross(small, large, message):
    return pl.pallas_call(
        cross_kernel,
        out_shape=jax.ShapeDtypeStruct((8, 4, 2, 72, 128), F32),
        in_specs=[
            pl.BlockSpec(memory_space=pltpu.HBM),
            pl.BlockSpec(memory_space=pltpu.HBM),
            pl.BlockSpec(memory_space=pl.ANY),
        ],
        out_specs=pl.BlockSpec(memory_space=pltpu.HBM),
        scratch_shapes=[
            pltpu.VMEM(small.shape, BF16),
            pltpu.VMEM(large.shape, BF16),
            pltpu.VMEM((2, 2, HALF, QUARTER), BF16),
            pltpu.VMEM((4, 2, 4, 72, 128), F32),
            pltpu.VMEM((8, 4, 2, 72, 128), F32),
            pltpu.VMEM((2, HALF, 256), F32),
            pltpu.VMEM((2, HALF, 256), F32),
            pltpu.VMEM((COUNT, 256), F32),
            pltpu.SemaphoreType.DMA((4,)),
            pltpu.SemaphoreType.DMA((2,)),
            pltpu.SemaphoreType.DMA((8,)),
        ],
        compiler_params=pltpu.CompilerParams(vmem_limit_bytes=60 * 2**20),
        cost_estimate=pl.CostEstimate(
            flops=3 * 2 * 3 * HALF * HALF * 256, bytes_accessed=12 * 2**20, transcendentals=0
        ),
    )(small, large, message.reshape(2, 4, 4, 72, 128))


def along_kernel(
    core_ref, table_ref, own, near, far_a, far_b, far_near_a, far_near_b, first_ref, second_ref
):
    core = core_ref[0]
    early = pl.program_id(0) == 0
    far = jnp.where(early, far_a[...], far_b[...])
    far_near = jnp.where(early, far_near_a[...], far_near_b[...])
    total = jnp.zeros((256, 2 * LANES), F32)
    pairs = ((own[...], 0), (near[...], 1 + 2 * core), (far, 2), (far_near, 3 - 2 * core))
    for block, r in pairs:
        high, low = split(block)
        total = total + three(high, low, table_ref[0, r], table_ref[1, r])
    first_ref[...] = total[:, :LANES]
    second_ref[...] = total[:, LANES:]


def along(core, table, *blocks):
    out = jax.ShapeDtypeStruct((ROWS * PLANES, LANES), F32)
    lines = pl.BlockSpec((256, LANES), lambda i, core: (i, 0))
    early = pl.BlockSpec((256, LANES), lambda i, core: (0, 0))
    late = pl.BlockSpec((256, LANES), lambda i, core: (jnp.maximum(i, 1) - 1, 0))
    return pl.pallas_call(
        along_kernel,
        grid_spec=pltpu.PrefetchScalarGridSpec(
            num_scalar_prefetch=1,
            grid=(3,),
            in_specs=[pl.BlockSpec((2, 4, LANES, 2 * LANES), lambda i, core: (0, 0, 0, 0))]
            + [lines, lines, early, late, early, late],
            out_specs=[lines] * 2,
        ),
        out_shape=(out, out),
        compiler_params=pltpu.CompilerParams(vmem_limit_bytes=24 * 2**20),
        cost_estimate=pl.CostEstimate(
            flops=2 * 3 * 768 * COUNT * 768, bytes_accessed=16 * 2**20, transcendentals=0
        ),
    )(core, table, *blocks)


def solution(mesh):
    fine = Mesh(mesh.devices.reshape(8, 4, 2, 2, 2), ("z", "y", "xl", "xh", "c"))
    small_t, large_t = cross_strips()
    along_t = along_table()
    pair = [(0, 1), (1, 0)]

    def swap(message):
        return lax.all_to_all(message, ("z", "y", "xl"), split_axis=0, concat_axis=0, tiled=True)

    def shards(moments):
        grid = moments.shape
        own = moments.reshape(ROWS * PLANES, LANES)
        far_a = lax.ppermute(own[:256], "xh", pair)
        near = lax.ppermute(own, "c", pair)
        home = swap(pack(moments.reshape(ROWS, PLANES, LANES)).reshape(64, 9, 4, 128))
        home, far_a, near = lax.optimization_barrier((home, far_a, near))
        far_b = lax.ppermute(own[256:], "xh", pair)
        back = swap(cross(jnp.asarray(small_t), jnp.asarray(large_t), home).reshape(64, 72, 128))
        far_near_a = lax.ppermute(far_a, "c", pair)
        far_near_b = lax.ppermute(far_b, "c", pair)
        core = lax.axis_index("c").reshape(1)
        first_z, second_z = along(
            core, jnp.asarray(along_t), own, near, far_a, far_b, far_near_a, far_near_b
        )
        first_z, second_z, back = lax.optimization_barrier((first_z, second_z, back))
        first, second = unpack(back.reshape(4608, 128))
        return (
            first.reshape(grid),
            second.reshape(grid),
            first_z.reshape(grid),
            second_z.reshape(grid),
        )

    spec = P(("z", "y", "xl"), None, None, ("xh", "c"))
    return jax.shard_map(
        shards, mesh=fine, in_specs=(spec,), out_specs=(spec,) * 4, check_vma=False
    )
```

```python
import math

import jax
import jax.numpy as jnp
import ml_dtypes
import numpy as np
from jax import lax
from jax.experimental import pallas as pl
from jax.experimental.pallas import tpu as pltpu
from jax.sharding import Mesh
from jax.sharding import PartitionSpec as P

COUNT = 1536
HALF = COUNT // 2
QUARTER = COUNT // 4
ROWS = 24
LANES = 384
PLANES = 32
F32 = jnp.float32
BF16 = jnp.bfloat16


def kernels():
    k = np.arange(COUNT, dtype=np.float64)
    sign = np.where(np.arange(COUNT) % 2 == 0, 1.0, -1.0)
    angle = math.pi * np.where(k == 0, 1.0, k) / COUNT
    first = np.where(k == 0, 0.0, math.pi / COUNT * sign / np.tan(angle))
    second = np.where(
        k == 0,
        -math.pi**2 / 3 - (2 * math.pi / COUNT) ** 2 / 6,
        -sign * (2 * math.pi**2 / COUNT**2) / np.sin(angle) ** 2,
    )
    return first, second


def halves(table):
    high = table.astype(ml_dtypes.bfloat16)
    low = (table - high.astype(np.float64)).astype(ml_dtypes.bfloat16)
    return np.stack([high, low])


def cross_strips():
    def strip(block, value):
        gap = 2 * block + np.arange(block)[:, None] - np.arange(5 * block)[None, :]
        return halves(np.stack([value(d, gap) for d in kernels()]))

    def plus(d, gap):
        return (d[gap % COUNT] + d[(gap + HALF) % COUNT]) / 2

    both = strip(128, lambda d, gap: (plus(d, gap) + plus(d, gap + QUARTER)) / 2)
    cross = strip(128, lambda d, gap: (plus(d, gap) - plus(d, gap + QUARTER)) / 2)
    minus = strip(256, lambda d, gap: (d[gap % COUNT] - d[(gap + HALF) % COUNT]) / 2)
    return np.stack([both, cross]), minus


def along_table():
    cell = np.arange(LANES)
    blocks = [
        np.concatenate(
            [d[(cell[None, :] - cell[:, None] - LANES * r) % COUNT] for d in kernels()], axis=1
        )
        for r in range(4)
    ]
    return halves(np.stack(blocks))


def split(value):
    high = value.astype(BF16)
    return high, (value - high.astype(F32)).astype(BF16)


def three(left_high, left_low, right_high, right_low):
    total = jnp.dot(left_high, right_high, preferred_element_type=F32)
    total = total + jnp.dot(left_high, right_low, preferred_element_type=F32)
    return total + jnp.dot(left_low, right_high, preferred_element_type=F32)


def low_lanes(shape):
    return lax.broadcasted_iota(jnp.int32, shape, len(shape) - 1) < 64


def pack_kernel(x_hbm, msg_hbm, x_ref, msg_ref, in_sems, out_sems):
    gets = [
        pltpu.make_async_copy(x_hbm.at[:, 8 * g : 8 * g + 8], x_ref.at[g], in_sems.at[g])
        for g in range(4)
    ]
    puts = [
        pltpu.make_async_copy(msg_ref.at[g], msg_hbm.at[576 * g : 576 * g + 576], out_sems.at[g])
        for g in range(4)
    ]
    near = low_lanes((8, 128))
    for get in gets:
        get.start()
    for g in range(4):
        gets[g].wait()
        for i in range(ROWS):
            for low in range(2):
                at = pl.ds(36 * low + i, 8, stride=72)
                msg_ref[g, at, :] = x_ref[g, i, :, 128 * low : 128 * low + 128]
        for i in range(12):
            top, bottom = x_ref[g, i, :, 256:384], x_ref[g, i + 12, :, 256:384]
            lower = jnp.where(near, top, pltpu.roll(bottom, 64, 1))
            upper = jnp.where(near, pltpu.roll(top, 64, 1), bottom)
            msg_ref[g, pl.ds(24 + i, 8, stride=72), :] = lower
            msg_ref[g, pl.ds(60 + i, 8, stride=72), :] = upper
        puts[g].start()
    for put in puts:
        put.wait()


def pack(block):
    return pl.pallas_call(
        pack_kernel,
        in_specs=[pl.BlockSpec(memory_space=pltpu.HBM)],
        out_specs=pl.BlockSpec(memory_space=pltpu.HBM),
        out_shape=jax.ShapeDtypeStruct((2304, 128), F32),
        scratch_shapes=[
            pltpu.VMEM((4, ROWS, 8, LANES), F32),
            pltpu.VMEM((4, 576, 128), F32),
            pltpu.SemaphoreType.DMA((4,)),
            pltpu.SemaphoreType.DMA((4,)),
        ],
        compiler_params=pltpu.CompilerParams(vmem_limit_bytes=56 * 2**20),
    )(block)


def unpack_kernel(msg_ref, first_hbm, second_hbm, out_ref, sems):
    near = low_lanes((8, 128))
    puts = []
    for g in range(4):
        base = 1152 * g
        for d, (out_hbm, full, part) in enumerate(((first_hbm, 0, 24), (second_hbm, 48, 36))):
            for i in range(ROWS):
                for low in range(2):
                    at = pl.ds(base + 72 * low + full + i, 8, stride=144)
                    out_ref[d, g, i, :, 128 * low : 128 * low + 128] = msg_ref[at, :]
            for i in range(12):
                lower = msg_ref[pl.ds(base + part + i, 8, stride=144), :]
                upper = msg_ref[pl.ds(base + 72 + part + i, 8, stride=144), :]
                out_ref[d, g, i, :, 256:384] = jnp.where(near, lower, pltpu.roll(upper, 64, 1))
                out_ref[d, g, i + 12, :, 256:384] = jnp.where(
                    near, pltpu.roll(lower, 64, 1), upper
                )
            put = pltpu.make_async_copy(
                out_ref.at[d, g], out_hbm.at[:, 8 * g : 8 * g + 8], sems.at[2 * g + d]
            )
            put.start()
            puts.append(put)
    for put in puts:
        put.wait()


def unpack(message):
    out = jax.ShapeDtypeStruct((ROWS, PLANES, LANES), F32)
    return pl.pallas_call(
        unpack_kernel,
        in_specs=[pl.BlockSpec(memory_space=pltpu.VMEM)],
        out_specs=[pl.BlockSpec(memory_space=pltpu.HBM)] * 2,
        out_shape=(out, out),
        scratch_shapes=[
            pltpu.VMEM((2, 4, ROWS, 8, LANES), F32),
            pltpu.SemaphoreType.DMA((8,)),
        ],
        compiler_params=pltpu.CompilerParams(vmem_limit_bytes=16 * 2**20),
    )(message)


def cross_kernel(
    token,
    small_hbm,
    large_hbm,
    msg,
    out_hbm,
    small_strip,
    large_strip,
    small,
    out,
    line,
    got_small,
    got_large,
    table_sems,
    out_sems,
):
    strips = [
        pltpu.make_async_copy(small_hbm, small_strip, table_sems.at[0]),
        pltpu.make_async_copy(large_hbm, large_strip, table_sems.at[1]),
    ]
    puts = [pltpu.make_async_copy(out.at[z], out_hbm.at[z], out_sems.at[z]) for z in range(8)]
    for copy in strips:
        copy.start()

    for c in range(4):
        for y in range(4):
            at = 48 * (4 * c + y)
            top, bottom = msg[0, c, y], msg[1, c, y]
            for k, value in enumerate((top + bottom, top - bottom)):
                line[k, at : at + 24, 0:128] = value[0:24]
                line[k, at + 24 : at + 48, 0:128] = value[36:60]
                even, odd = value[24:36], value[60:72]
                parts = [even, pltpu.roll(even, 64, 1), odd, pltpu.roll(odd, 64, 1)]
                line[k, at : at + 48, 128:256] = jnp.concatenate(parts, axis=0)

    for copy in strips:
        copy.wait()
    for h in range(2):
        for d in range(2):
            for i in range(3):
                rows = slice(QUARTER * d + 128 * i, QUARTER * d + 128 * i + 128)
                lanes = slice(128 * (2 - i), 128 * (2 - i) + QUARTER)
                for k in range(2):
                    small[k, h, rows, :] = small_strip[k, h, d, :, lanes]
    head, tail = line[0, :QUARTER, :], line[0, QUARTER:, :]
    for k, value in enumerate((head + tail, head - tail)):
        high, low = split(value)
        got_small[k] = three(small[k, 0], small[k, 1], high, low)

    high, low = split(line[1])
    near = low_lanes((12, 128))

    def products(i):
        for d in range(2):
            lanes = slice(256 * (2 - i), 256 * (2 - i) + HALF)
            left = large_strip[0, d, :, lanes], large_strip[1, d, :, lanes]
            got_large[HALF * d + 256 * i : HALF * d + 256 * i + 256, :] = three(*left, high, low)

    def close(c):
        for y in range(4):
            for part_of in range(2):
                at = 48 * (4 * c + y) + ROWS * part_of
                for d, (full, part) in enumerate(((0, 24), (48, 36))):
                    minus = got_large[HALF * d + at : HALF * d + at + ROWS, :]
                    place = QUARTER * d + at % QUARTER
                    one = got_small[0, place : place + ROWS, :]
                    two = got_small[1, place : place + ROWS, :]
                    plus = one + two if at < QUARTER else one - two
                    for z, value in ((c, plus + minus), (c + 4, plus - minus)):
                        out[z, y, part_of, full : full + 24] = value[:, 0:128]
                        top, bottom = value[:12, 128:256], value[12:, 128:256]
                        out[z, y, part_of, part : part + 12] = jnp.where(
                            near, top, pltpu.roll(bottom, 64, 1)
                        )
        puts[c].start()
        puts[c + 4].start()

    products(0)
    products(1)
    close(0)
    products(2)
    close(1)
    close(2)
    close(3)
    for put in puts:
        put.wait()


def cross(token, small, large, message):
    return pl.pallas_call(
        cross_kernel,
        out_shape=jax.ShapeDtypeStruct((8, 4, 2, 72, 128), F32),
        in_specs=[
            pl.BlockSpec(memory_space=pltpu.SMEM),
            pl.BlockSpec(memory_space=pltpu.HBM),
            pl.BlockSpec(memory_space=pltpu.HBM),
            pl.BlockSpec(memory_space=pltpu.VMEM),
        ],
        out_specs=pl.BlockSpec(memory_space=pltpu.HBM),
        scratch_shapes=[
            pltpu.VMEM(small.shape, BF16),
            pltpu.VMEM(large.shape, BF16),
            pltpu.VMEM((2, 2, HALF, QUARTER), BF16),
            pltpu.VMEM((8, 4, 2, 72, 128), F32),
            pltpu.VMEM((2, HALF, 256), F32),
            pltpu.VMEM((2, HALF, 256), F32),
            pltpu.VMEM((COUNT, 256), F32),
            pltpu.SemaphoreType.DMA((2,)),
            pltpu.SemaphoreType.DMA((8,)),
        ],
        compiler_params=pltpu.CompilerParams(vmem_limit_bytes=56 * 2**20),
        cost_estimate=pl.CostEstimate(
            flops=3 * 2 * 3 * HALF * HALF * 256, bytes_accessed=12 * 2**20, transcendentals=0
        ),
    )(token, small, large, message.reshape(2, 4, 4, 72, 128))


def along_kernel(
    core_ref, table_ref, own, near, far_a, far_b, far_near_a, far_near_b, first_ref, second_ref
):
    core = core_ref[0]
    early = pl.program_id(0) == 0
    far = jnp.where(early, far_a[...], far_b[...])
    far_near = jnp.where(early, far_near_a[...], far_near_b[...])
    total = jnp.zeros((256, 2 * LANES), F32)
    pairs = ((own[...], 0), (near[...], 1 + 2 * core), (far, 2), (far_near, 3 - 2 * core))
    for block, r in pairs:
        high, low = split(block)
        total = total + three(high, low, table_ref[0, r], table_ref[1, r])
    first_ref[...] = total[:, :LANES]
    second_ref[...] = total[:, LANES:]


def along(core, table, *blocks):
    out = jax.ShapeDtypeStruct((ROWS * PLANES, LANES), F32)
    lines = pl.BlockSpec((256, LANES), lambda i, core: (i, 0))
    early = pl.BlockSpec((256, LANES), lambda i, core: (0, 0))
    late = pl.BlockSpec((256, LANES), lambda i, core: (jnp.maximum(i, 1) - 1, 0))
    return pl.pallas_call(
        along_kernel,
        grid_spec=pltpu.PrefetchScalarGridSpec(
            num_scalar_prefetch=1,
            grid=(3,),
            in_specs=[pl.BlockSpec((2, 4, LANES, 2 * LANES), lambda i, core: (0, 0, 0, 0))]
            + [lines, lines, early, late, early, late],
            out_specs=[lines] * 2,
        ),
        out_shape=(out, out),
        compiler_params=pltpu.CompilerParams(vmem_limit_bytes=24 * 2**20),
        cost_estimate=pl.CostEstimate(
            flops=2 * 3 * 768 * COUNT * 768, bytes_accessed=16 * 2**20, transcendentals=0
        ),
    )(core, table, *blocks)


def solution(mesh):
    fine = Mesh(mesh.devices.reshape(8, 4, 2, 2, 2), ("z", "y", "xl", "xh", "c"))
    small_t, large_t = cross_strips()
    along_t = along_table()
    pair = [(0, 1), (1, 0)]

    def swap(message):
        return lax.all_to_all(message, ("z", "y", "xl"), split_axis=0, concat_axis=0, tiled=True)

    def shards(moments):
        grid = moments.shape
        own = moments.reshape(ROWS * PLANES, LANES)
        far_a = lax.ppermute(own[:256], "xh", pair)
        near = lax.ppermute(own, "c", pair)
        home = swap(pack(moments.reshape(ROWS, PLANES, LANES)).reshape(64, 9, 4, 128))
        token = jnp.zeros((1,), jnp.int32)
        token, far_a, near = lax.optimization_barrier((token, far_a, near))
        far_b = lax.ppermute(own[256:], "xh", pair)
        results = cross(token, jnp.asarray(small_t), jnp.asarray(large_t), home)
        back = swap(results.reshape(64, 72, 128))
        far_near_a = lax.ppermute(far_a, "c", pair)
        far_near_b = lax.ppermute(far_b, "c", pair)
        core = lax.axis_index("c").reshape(1)
        first_z, second_z = along(
            core, jnp.asarray(along_t), own, near, far_a, far_b, far_near_a, far_near_b
        )
        first_z, second_z, back = lax.optimization_barrier((first_z, second_z, back))
        first, second = unpack(back.reshape(4608, 128))
        return (
            first.reshape(grid),
            second.reshape(grid),
            first_z.reshape(grid),
            second_z.reshape(grid),
        )

    spec = P(("z", "y", "xl"), None, None, ("xh", "c"))
    return jax.shard_map(
        shards, mesh=fine, in_specs=(spec,), out_specs=(spec,) * 4, check_vma=False
    )
```

```python
import math

import jax
import jax.numpy as jnp
import ml_dtypes
import numpy as np
from jax import lax
from jax.experimental import pallas as pl
from jax.experimental.pallas import tpu as pltpu
from jax.sharding import Mesh
from jax.sharding import PartitionSpec as P

COUNT = 1536
HALF = COUNT // 2
QUARTER = COUNT // 4
ROWS = 24
LANES = 384
PLANES = 32
F32 = jnp.float32
BF16 = jnp.bfloat16


def kernels():
    k = np.arange(COUNT, dtype=np.float64)
    sign = np.where(np.arange(COUNT) % 2 == 0, 1.0, -1.0)
    angle = math.pi * np.where(k == 0, 1.0, k) / COUNT
    first = np.where(k == 0, 0.0, math.pi / COUNT * sign / np.tan(angle))
    second = np.where(
        k == 0,
        -math.pi**2 / 3 - (2 * math.pi / COUNT) ** 2 / 6,
        -sign * (2 * math.pi**2 / COUNT**2) / np.sin(angle) ** 2,
    )
    return first, second


def halves(table):
    high = table.astype(ml_dtypes.bfloat16)
    low = (table - high.astype(np.float64)).astype(ml_dtypes.bfloat16)
    return np.stack([high, low])


def cross_strips():
    def strip(block, value):
        gap = 2 * block + np.arange(block)[:, None] - np.arange(5 * block)[None, :]
        return halves(np.stack([value(d, gap) for d in kernels()]))

    def plus(d, gap):
        return (d[gap % COUNT] + d[(gap + HALF) % COUNT]) / 2

    both = strip(128, lambda d, gap: (plus(d, gap) + plus(d, gap + QUARTER)) / 2)
    cross = strip(128, lambda d, gap: (plus(d, gap) - plus(d, gap + QUARTER)) / 2)
    minus = strip(256, lambda d, gap: (d[gap % COUNT] - d[(gap + HALF) % COUNT]) / 2)
    return np.stack([both, cross]), minus


def along_table():
    cell = np.arange(LANES)
    blocks = [
        np.concatenate(
            [d[(cell[None, :] - cell[:, None] - LANES * r) % COUNT] for d in kernels()], axis=1
        )
        for r in range(4)
    ]
    return halves(np.stack(blocks))


def split(value):
    high = value.astype(BF16)
    return high, (value - high.astype(F32)).astype(BF16)


def three(left_high, left_low, right_high, right_low):
    total = jnp.dot(left_high, right_high, preferred_element_type=F32)
    total = total + jnp.dot(left_high, right_low, preferred_element_type=F32)
    return total + jnp.dot(left_low, right_high, preferred_element_type=F32)


def low_lanes(shape):
    return lax.broadcasted_iota(jnp.int32, shape, len(shape) - 1) < 64


def pack_kernel(x_hbm, msg_hbm, x_ref, msg_ref, in_sems, out_sems):
    gets = [
        [
            pltpu.make_async_copy(
                x_hbm.at[12 * part : 12 * part + 12, 8 * g : 8 * g + 8],
                x_ref.at[g, 12 * part : 12 * part + 12],
                in_sems.at[2 * g + part],
            )
            for part in range(2)
        ]
        for g in range(4)
    ]
    puts = [
        [
            pltpu.make_async_copy(
                msg_ref.at[g, 288 * part : 288 * part + 288],
                msg_hbm.at[576 * g + 288 * part : 576 * g + 288 * part + 288],
                out_sems.at[2 * g + part],
            )
            for part in range(2)
        ]
        for g in range(4)
    ]
    near = low_lanes((8, 128))
    for get in sum(gets, []):
        get.start()
    for g in range(4):
        for get in gets[g]:
            get.wait()
        for i in range(ROWS):
            for low in range(2):
                at = pl.ds(36 * low + i, 8, stride=72)
                msg_ref[g, at, :] = x_ref[g, i, :, 128 * low : 128 * low + 128]
        for i in range(12):
            top, bottom = x_ref[g, i, :, 256:384], x_ref[g, i + 12, :, 256:384]
            lower = jnp.where(near, top, pltpu.roll(bottom, 64, 1))
            upper = jnp.where(near, pltpu.roll(top, 64, 1), bottom)
            msg_ref[g, pl.ds(24 + i, 8, stride=72), :] = lower
            msg_ref[g, pl.ds(60 + i, 8, stride=72), :] = upper
        for put in puts[g]:
            put.start()
    for put in sum(puts, []):
        put.wait()


def pack(block):
    return pl.pallas_call(
        pack_kernel,
        in_specs=[pl.BlockSpec(memory_space=pltpu.HBM)],
        out_specs=pl.BlockSpec(memory_space=pltpu.HBM),
        out_shape=jax.ShapeDtypeStruct((2304, 128), F32),
        scratch_shapes=[
            pltpu.VMEM((4, ROWS, 8, LANES), F32),
            pltpu.VMEM((4, 576, 128), F32),
            pltpu.SemaphoreType.DMA((8,)),
            pltpu.SemaphoreType.DMA((8,)),
        ],
        compiler_params=pltpu.CompilerParams(vmem_limit_bytes=56 * 2**20),
    )(block)


def unpack_kernel(msg_ref, first_hbm, second_hbm, out_ref, sems):
    near = low_lanes((8, 128))
    puts = []
    for g in range(4):
        base = 1152 * g
        for d, (out_hbm, full, part) in enumerate(((first_hbm, 0, 24), (second_hbm, 48, 36))):
            for i in range(ROWS):
                for low in range(2):
                    at = pl.ds(base + 72 * low + full + i, 8, stride=144)
                    out_ref[d, g, i, :, 128 * low : 128 * low + 128] = msg_ref[at, :]
            for i in range(12):
                lower = msg_ref[pl.ds(base + part + i, 8, stride=144), :]
                upper = msg_ref[pl.ds(base + 72 + part + i, 8, stride=144), :]
                out_ref[d, g, i, :, 256:384] = jnp.where(near, lower, pltpu.roll(upper, 64, 1))
                out_ref[d, g, i + 12, :, 256:384] = jnp.where(
                    near, pltpu.roll(lower, 64, 1), upper
                )
            put = pltpu.make_async_copy(
                out_ref.at[d, g], out_hbm.at[:, 8 * g : 8 * g + 8], sems.at[2 * g + d]
            )
            put.start()
            puts.append(put)
    for put in puts:
        put.wait()


def unpack(message):
    out = jax.ShapeDtypeStruct((ROWS, PLANES, LANES), F32)
    return pl.pallas_call(
        unpack_kernel,
        in_specs=[pl.BlockSpec(memory_space=pltpu.VMEM)],
        out_specs=[pl.BlockSpec(memory_space=pltpu.HBM)] * 2,
        out_shape=(out, out),
        scratch_shapes=[
            pltpu.VMEM((2, 4, ROWS, 8, LANES), F32),
            pltpu.SemaphoreType.DMA((8,)),
        ],
        compiler_params=pltpu.CompilerParams(vmem_limit_bytes=16 * 2**20),
    )(message)


def cross_kernel(
    small_hbm,
    large_hbm,
    msg_hbm,
    out_hbm,
    small_strip,
    large_strip,
    small,
    msg,
    out,
    line,
    got_small,
    got_large,
    in_sems,
    table_sems,
    out_sems,
):
    gets = [
        [
            pltpu.make_async_copy(msg_hbm.at[side, c], msg.at[c, side], in_sems.at[2 * c + side])
            for side in range(2)
        ]
        for c in range(4)
    ]
    small_loads = [
        pltpu.make_async_copy(
            small_hbm.at[k, h], small_strip.at[k, h], table_sems.at[2 * k + h]
        )
        for k in range(2)
        for h in range(2)
    ]
    large_loads = [
        pltpu.make_async_copy(
            large_hbm.at[h, d], large_strip.at[h, d], table_sems.at[4 + 2 * h + d]
        )
        for h in range(2)
        for d in range(2)
    ]
    puts = [pltpu.make_async_copy(out.at[z], out_hbm.at[z], out_sems.at[z]) for z in range(8)]
    for copy in sum(gets, []) + small_loads + large_loads:
        copy.start()

    for c in range(4):
        for get in gets[c]:
            get.wait()
        for y in range(4):
            at = 48 * (4 * c + y)
            top, bottom = msg[c, 0, y], msg[c, 1, y]
            for k, value in enumerate((top + bottom, top - bottom)):
                line[k, at : at + 24, 0:128] = value[0:24]
                line[k, at + 24 : at + 48, 0:128] = value[36:60]
                even, odd = value[24:36], value[60:72]
                parts = [even, pltpu.roll(even, 64, 1), odd, pltpu.roll(odd, 64, 1)]
                line[k, at : at + 48, 128:256] = jnp.concatenate(parts, axis=0)

    for copy in small_loads:
        copy.wait()
    for h in range(2):
        for d in range(2):
            for i in range(3):
                rows = slice(QUARTER * d + 128 * i, QUARTER * d + 128 * i + 128)
                lanes = slice(128 * (2 - i), 128 * (2 - i) + QUARTER)
                for k in range(2):
                    small[k, h, rows, :] = small_strip[k, h, d, :, lanes]
    head, tail = line[0, :QUARTER, :], line[0, QUARTER:, :]
    for k, value in enumerate((head + tail, head - tail)):
        high, low = split(value)
        got_small[k] = three(small[k, 0], small[k, 1], high, low)

    high, low = split(line[1])
    for copy in large_loads:
        copy.wait()
    near = low_lanes((12, 128))

    def products(i):
        for d in range(2):
            lanes = slice(256 * (2 - i), 256 * (2 - i) + HALF)
            left = large_strip[0, d, :, lanes], large_strip[1, d, :, lanes]
            got_large[HALF * d + 256 * i : HALF * d + 256 * i + 256, :] = three(*left, high, low)

    def close(c):
        for y in range(4):
            for part_of in range(2):
                at = 48 * (4 * c + y) + ROWS * part_of
                for d, (full, part) in enumerate(((0, 24), (48, 36))):
                    minus = got_large[HALF * d + at : HALF * d + at + ROWS, :]
                    place = QUARTER * d + at % QUARTER
                    one = got_small[0, place : place + ROWS, :]
                    two = got_small[1, place : place + ROWS, :]
                    plus = one + two if at < QUARTER else one - two
                    for z, value in ((c, plus + minus), (c + 4, plus - minus)):
                        out[z, y, part_of, full : full + 24] = value[:, 0:128]
                        top, bottom = value[:12, 128:256], value[12:, 128:256]
                        out[z, y, part_of, part : part + 12] = jnp.where(
                            near, top, pltpu.roll(bottom, 64, 1)
                        )
        puts[c].start()
        puts[c + 4].start()

    products(0)
    products(1)
    close(0)
    products(2)
    close(1)
    close(2)
    close(3)
    for put in puts:
        put.wait()


def cross(small, large, message):
    return pl.pallas_call(
        cross_kernel,
        out_shape=jax.ShapeDtypeStruct((8, 4, 2, 72, 128), F32),
        in_specs=[
            pl.BlockSpec(memory_space=pltpu.HBM),
            pl.BlockSpec(memory_space=pltpu.HBM),
            pl.BlockSpec(memory_space=pl.ANY),
        ],
        out_specs=pl.BlockSpec(memory_space=pltpu.HBM),
        scratch_shapes=[
            pltpu.VMEM(small.shape, BF16),
            pltpu.VMEM(large.shape, BF16),
            pltpu.VMEM((2, 2, HALF, QUARTER), BF16),
            pltpu.VMEM((4, 2, 4, 72, 128), F32),
            pltpu.VMEM((8, 4, 2, 72, 128), F32),
            pltpu.VMEM((2, HALF, 256), F32),
            pltpu.VMEM((2, HALF, 256), F32),
            pltpu.VMEM((COUNT, 256), F32),
            pltpu.SemaphoreType.DMA((8,)),
            pltpu.SemaphoreType.DMA((8,)),
            pltpu.SemaphoreType.DMA((8,)),
        ],
        compiler_params=pltpu.CompilerParams(vmem_limit_bytes=60 * 2**20),
        cost_estimate=pl.CostEstimate(
            flops=3 * 2 * 3 * HALF * HALF * 256, bytes_accessed=12 * 2**20, transcendentals=0
        ),
    )(small, large, message.reshape(2, 4, 4, 72, 128))


def along_kernel(
    core_ref, table_ref, own, near, far_a, far_b, far_near_a, far_near_b, first_ref, second_ref
):
    core = core_ref[0]
    early = pl.program_id(0) == 0
    far = jnp.where(early, far_a[...], far_b[...])
    far_near = jnp.where(early, far_near_a[...], far_near_b[...])
    total = jnp.zeros((256, 2 * LANES), F32)
    pairs = ((own[...], 0), (near[...], 1 + 2 * core), (far, 2), (far_near, 3 - 2 * core))
    for block, r in pairs:
        high, low = split(block)
        total = total + three(high, low, table_ref[0, r], table_ref[1, r])
    first_ref[...] = total[:, :LANES]
    second_ref[...] = total[:, LANES:]


def along(core, table, *blocks):
    out = jax.ShapeDtypeStruct((ROWS * PLANES, LANES), F32)
    lines = pl.BlockSpec((256, LANES), lambda i, core: (i, 0))
    early = pl.BlockSpec((256, LANES), lambda i, core: (0, 0))
    late = pl.BlockSpec((256, LANES), lambda i, core: (jnp.maximum(i, 1) - 1, 0))
    return pl.pallas_call(
        along_kernel,
        grid_spec=pltpu.PrefetchScalarGridSpec(
            num_scalar_prefetch=1,
            grid=(3,),
            in_specs=[pl.BlockSpec((2, 4, LANES, 2 * LANES), lambda i, core: (0, 0, 0, 0))]
            + [lines, lines, early, late, early, late],
            out_specs=[lines] * 2,
        ),
        out_shape=(out, out),
        compiler_params=pltpu.CompilerParams(vmem_limit_bytes=24 * 2**20),
        cost_estimate=pl.CostEstimate(
            flops=2 * 3 * 768 * COUNT * 768, bytes_accessed=16 * 2**20, transcendentals=0
        ),
    )(core, table, *blocks)


def solution(mesh):
    fine = Mesh(mesh.devices.reshape(8, 4, 2, 2, 2), ("z", "y", "xl", "xh", "c"))
    small_t, large_t = cross_strips()
    along_t = along_table()
    pair = [(0, 1), (1, 0)]

    def swap(message):
        return lax.all_to_all(message, ("z", "y", "xl"), split_axis=0, concat_axis=0, tiled=True)

    def shards(moments):
        grid = moments.shape
        own = moments.reshape(ROWS * PLANES, LANES)
        far_a = lax.ppermute(own[:256], "xh", pair)
        near = lax.ppermute(own, "c", pair)
        home = swap(pack(moments.reshape(ROWS, PLANES, LANES)).reshape(64, 9, 4, 128))
        home, far_a, near = lax.optimization_barrier((home, far_a, near))
        far_b = lax.ppermute(own[256:], "xh", pair)
        back = swap(cross(jnp.asarray(small_t), jnp.asarray(large_t), home).reshape(64, 72, 128))
        far_near_a = lax.ppermute(far_a, "c", pair)
        far_near_b = lax.ppermute(far_b, "c", pair)
        core = lax.axis_index("c").reshape(1)
        first_z, second_z = along(
            core, jnp.asarray(along_t), own, near, far_a, far_b, far_near_a, far_near_b
        )
        first_z, second_z, back = lax.optimization_barrier((first_z, second_z, back))
        first, second = unpack(back.reshape(4608, 128))
        return (
            first.reshape(grid),
            second.reshape(grid),
            first_z.reshape(grid),
            second_z.reshape(grid),
        )

    spec = P(("z", "y", "xl"), None, None, ("xh", "c"))
    return jax.shard_map(
        shards, mesh=fine, in_specs=(spec,), out_specs=(spec,) * 4, check_vma=False
    )
```

```python
import math

import jax
import jax.numpy as jnp
import ml_dtypes
import numpy as np
from jax import lax
from jax.experimental import pallas as pl
from jax.experimental.pallas import tpu as pltpu
from jax.sharding import Mesh
from jax.sharding import PartitionSpec as P

COUNT = 1536
HALF = COUNT // 2
QUARTER = COUNT // 4
ROWS = 24
LANES = 384
PLANES = 32
F32 = jnp.float32
BF16 = jnp.bfloat16


def kernels():
    k = np.arange(COUNT, dtype=np.float64)
    sign = np.where(np.arange(COUNT) % 2 == 0, 1.0, -1.0)
    angle = math.pi * np.where(k == 0, 1.0, k) / COUNT
    first = np.where(k == 0, 0.0, math.pi / COUNT * sign / np.tan(angle))
    second = np.where(
        k == 0,
        -math.pi**2 / 3 - (2 * math.pi / COUNT) ** 2 / 6,
        -sign * (2 * math.pi**2 / COUNT**2) / np.sin(angle) ** 2,
    )
    return first, second


def halves(table):
    high = table.astype(ml_dtypes.bfloat16)
    low = (table - high.astype(np.float64)).astype(ml_dtypes.bfloat16)
    return np.stack([high, low])


def cross_strips():
    def strip(block, value):
        gap = 2 * block + np.arange(block)[:, None] - np.arange(5 * block)[None, :]
        return halves(np.stack([value(d, gap) for d in kernels()]))

    def plus(d, gap):
        return (d[gap % COUNT] + d[(gap + HALF) % COUNT]) / 2

    both = strip(128, lambda d, gap: (plus(d, gap) + plus(d, gap + QUARTER)) / 2)
    cross = strip(128, lambda d, gap: (plus(d, gap) - plus(d, gap + QUARTER)) / 2)
    minus = strip(256, lambda d, gap: (d[gap % COUNT] - d[(gap + HALF) % COUNT]) / 2)
    return np.stack([both, cross]), minus


def along_table():
    cell = np.arange(LANES)
    blocks = [
        np.concatenate(
            [d[(cell[None, :] - cell[:, None] - LANES * r) % COUNT] for d in kernels()], axis=1
        )
        for r in range(4)
    ]
    return halves(np.stack(blocks))


def split(value):
    high = value.astype(BF16)
    return high, (value - high.astype(F32)).astype(BF16)


def three(left_high, left_low, right_high, right_low):
    total = jnp.dot(left_high, right_high, preferred_element_type=F32)
    total = total + jnp.dot(left_high, right_low, preferred_element_type=F32)
    return total + jnp.dot(left_low, right_high, preferred_element_type=F32)


def low_lanes(shape):
    return lax.broadcasted_iota(jnp.int32, shape, len(shape) - 1) < 64


def pack_kernel(x_hbm, msg_hbm, x_ref, msg_ref, in_sems, out_sems):
    gets = [
        pltpu.make_async_copy(x_hbm.at[:, 8 * g : 8 * g + 8], x_ref.at[g], in_sems.at[g])
        for g in range(4)
    ]
    puts = [
        pltpu.make_async_copy(msg_ref.at[g], msg_hbm.at[576 * g : 576 * g + 576], out_sems.at[g])
        for g in range(4)
    ]
    near = low_lanes((8, 128))
    for get in gets:
        get.start()
    for g in range(4):
        gets[g].wait()
        for i in range(ROWS):
            for low in range(2):
                at = pl.ds(36 * low + i, 8, stride=72)
                msg_ref[g, at, :] = x_ref[g, i, :, 128 * low : 128 * low + 128]
        for i in range(12):
            top, bottom = x_ref[g, i, :, 256:384], x_ref[g, i + 12, :, 256:384]
            lower = jnp.where(near, top, pltpu.roll(bottom, 64, 1))
            upper = jnp.where(near, pltpu.roll(top, 64, 1), bottom)
            msg_ref[g, pl.ds(24 + i, 8, stride=72), :] = lower
            msg_ref[g, pl.ds(60 + i, 8, stride=72), :] = upper
        puts[g].start()
    for put in puts:
        put.wait()


def pack(block):
    return pl.pallas_call(
        pack_kernel,
        in_specs=[pl.BlockSpec(memory_space=pltpu.HBM)],
        out_specs=pl.BlockSpec(memory_space=pltpu.HBM),
        out_shape=jax.ShapeDtypeStruct((2304, 128), F32),
        scratch_shapes=[
            pltpu.VMEM((4, ROWS, 8, LANES), F32),
            pltpu.VMEM((4, 576, 128), F32),
            pltpu.SemaphoreType.DMA((4,)),
            pltpu.SemaphoreType.DMA((4,)),
        ],
        compiler_params=pltpu.CompilerParams(vmem_limit_bytes=56 * 2**20),
    )(block)


def unpack_kernel(msg_ref, first_hbm, second_hbm, out_ref, sems):
    near = low_lanes((8, 128))
    puts = []
    for g in range(4):
        base = 1152 * g
        for d, (out_hbm, full, part) in enumerate(((first_hbm, 0, 24), (second_hbm, 48, 36))):
            for i in range(ROWS):
                for low in range(2):
                    at = pl.ds(base + 72 * low + full + i, 8, stride=144)
                    out_ref[d, g, i, :, 128 * low : 128 * low + 128] = msg_ref[at, :]
            for i in range(12):
                lower = msg_ref[pl.ds(base + part + i, 8, stride=144), :]
                upper = msg_ref[pl.ds(base + 72 + part + i, 8, stride=144), :]
                out_ref[d, g, i, :, 256:384] = jnp.where(near, lower, pltpu.roll(upper, 64, 1))
                out_ref[d, g, i + 12, :, 256:384] = jnp.where(
                    near, pltpu.roll(lower, 64, 1), upper
                )
            put = pltpu.make_async_copy(
                out_ref.at[d, g], out_hbm.at[:, 8 * g : 8 * g + 8], sems.at[2 * g + d]
            )
            put.start()
            puts.append(put)
    for put in puts:
        put.wait()


def unpack(message):
    out = jax.ShapeDtypeStruct((ROWS, PLANES, LANES), F32)
    return pl.pallas_call(
        unpack_kernel,
        in_specs=[pl.BlockSpec(memory_space=pltpu.VMEM)],
        out_specs=[pl.BlockSpec(memory_space=pltpu.HBM)] * 2,
        out_shape=(out, out),
        scratch_shapes=[
            pltpu.VMEM((2, 4, ROWS, 8, LANES), F32),
            pltpu.SemaphoreType.DMA((8,)),
        ],
        compiler_params=pltpu.CompilerParams(vmem_limit_bytes=16 * 2**20),
    )(message)


def cross_kernel(
    small_hbm,
    large_hbm,
    msg_hbm,
    out_hbm,
    small_strip,
    large_strip,
    small,
    msg,
    out,
    line,
    got_small,
    got_large,
    in_sems,
    table_sems,
    out_sems,
):
    gets = [
        pltpu.make_async_copy(msg_hbm.at[:, :, c], msg.at[c], in_sems.at[c]) for c in range(4)
    ]
    strips = [
        pltpu.make_async_copy(small_hbm, small_strip, table_sems.at[0]),
        pltpu.make_async_copy(large_hbm, large_strip, table_sems.at[1]),
    ]
    puts = [pltpu.make_async_copy(out.at[z], out_hbm.at[:, z], out_sems.at[z]) for z in range(8)]
    for copy in gets + strips:
        copy.start()

    for c in range(4):
        gets[c].wait()
        for y in range(4):
            at = 48 * (4 * c + y)
            top, bottom = msg[c, y, 0], msg[c, y, 1]
            for k, value in enumerate((top + bottom, top - bottom)):
                line[k, at : at + 24, 0:128] = value[0:24]
                line[k, at + 24 : at + 48, 0:128] = value[36:60]
                even, odd = value[24:36], value[60:72]
                parts = [even, pltpu.roll(even, 64, 1), odd, pltpu.roll(odd, 64, 1)]
                line[k, at : at + 48, 128:256] = jnp.concatenate(parts, axis=0)

    for copy in strips:
        copy.wait()
    for h in range(2):
        for d in range(2):
            for i in range(3):
                rows = slice(QUARTER * d + 128 * i, QUARTER * d + 128 * i + 128)
                lanes = slice(128 * (2 - i), 128 * (2 - i) + QUARTER)
                for k in range(2):
                    small[k, h, rows, :] = small_strip[k, h, d, :, lanes]
    head, tail = line[0, :QUARTER, :], line[0, QUARTER:, :]
    for k, value in enumerate((head + tail, head - tail)):
        high, low = split(value)
        got_small[k] = three(small[k, 0], small[k, 1], high, low)

    high, low = split(line[1])
    near = low_lanes((12, 128))

    def products(i):
        for d in range(2):
            lanes = slice(256 * (2 - i), 256 * (2 - i) + HALF)
            left = large_strip[0, d, :, lanes], large_strip[1, d, :, lanes]
            got_large[HALF * d + 256 * i : HALF * d + 256 * i + 256, :] = three(*left, high, low)

    def close(c):
        for y in range(4):
            for part_of in range(2):
                at = 48 * (4 * c + y) + ROWS * part_of
                for d, (full, part) in enumerate(((0, 24), (48, 36))):
                    minus = got_large[HALF * d + at : HALF * d + at + ROWS, :]
                    place = QUARTER * d + at % QUARTER
                    one = got_small[0, place : place + ROWS, :]
                    two = got_small[1, place : place + ROWS, :]
                    plus = one + two if at < QUARTER else one - two
                    for z, value in ((c, plus + minus), (c + 4, plus - minus)):
                        out[z, y, part_of, full : full + 24] = value[:, 0:128]
                        top, bottom = value[:12, 128:256], value[12:, 128:256]
                        out[z, y, part_of, part : part + 12] = jnp.where(
                            near, top, pltpu.roll(bottom, 64, 1)
                        )
        puts[c].start()
        puts[c + 4].start()

    products(0)
    products(1)
    close(0)
    products(2)
    close(1)
    close(2)
    close(3)
    for put in puts:
        put.wait()


def cross(small, large, message):
    return pl.pallas_call(
        cross_kernel,
        out_shape=jax.ShapeDtypeStruct((4, 8, 2, 72, 128), F32),
        in_specs=[
            pl.BlockSpec(memory_space=pltpu.HBM),
            pl.BlockSpec(memory_space=pltpu.HBM),
            pl.BlockSpec(memory_space=pl.ANY),
        ],
        out_specs=pl.BlockSpec(memory_space=pltpu.HBM),
        scratch_shapes=[
            pltpu.VMEM(small.shape, BF16),
            pltpu.VMEM(large.shape, BF16),
            pltpu.VMEM((2, 2, HALF, QUARTER), BF16),
            pltpu.VMEM((4, 4, 2, 72, 128), F32),
            pltpu.VMEM((8, 4, 2, 72, 128), F32),
            pltpu.VMEM((2, HALF, 256), F32),
            pltpu.VMEM((2, HALF, 256), F32),
            pltpu.VMEM((COUNT, 256), F32),
            pltpu.SemaphoreType.DMA((4,)),
            pltpu.SemaphoreType.DMA((2,)),
            pltpu.SemaphoreType.DMA((8,)),
        ],
        compiler_params=pltpu.CompilerParams(vmem_limit_bytes=60 * 2**20),
        cost_estimate=pl.CostEstimate(
            flops=3 * 2 * 3 * HALF * HALF * 256, bytes_accessed=12 * 2**20, transcendentals=0
        ),
    )(small, large, message.reshape(4, 2, 4, 72, 128))


def along_kernel(
    core_ref, table_ref, own, near, far_a, far_b, far_near_a, far_near_b, first_ref, second_ref
):
    core = core_ref[0]
    early = pl.program_id(0) == 0
    far = jnp.where(early, far_a[...], far_b[...])
    far_near = jnp.where(early, far_near_a[...], far_near_b[...])
    total = jnp.zeros((256, 2 * LANES), F32)
    pairs = ((own[...], 0), (near[...], 1 + 2 * core), (far, 2), (far_near, 3 - 2 * core))
    for block, r in pairs:
        high, low = split(block)
        total = total + three(high, low, table_ref[0, r], table_ref[1, r])
    first_ref[...] = total[:, :LANES]
    second_ref[...] = total[:, LANES:]


def along(core, table, *blocks):
    out = jax.ShapeDtypeStruct((ROWS * PLANES, LANES), F32)
    lines = pl.BlockSpec((256, LANES), lambda i, core: (i, 0))
    early = pl.BlockSpec((256, LANES), lambda i, core: (0, 0))
    late = pl.BlockSpec((256, LANES), lambda i, core: (jnp.maximum(i, 1) - 1, 0))
    return pl.pallas_call(
        along_kernel,
        grid_spec=pltpu.PrefetchScalarGridSpec(
            num_scalar_prefetch=1,
            grid=(3,),
            in_specs=[pl.BlockSpec((2, 4, LANES, 2 * LANES), lambda i, core: (0, 0, 0, 0))]
            + [lines, lines, early, late, early, late],
            out_specs=[lines] * 2,
        ),
        out_shape=(out, out),
        compiler_params=pltpu.CompilerParams(vmem_limit_bytes=24 * 2**20),
        cost_estimate=pl.CostEstimate(
            flops=2 * 3 * 768 * COUNT * 768, bytes_accessed=16 * 2**20, transcendentals=0
        ),
    )(core, table, *blocks)


def solution(mesh):
    fine = Mesh(mesh.devices.reshape(8, 4, 2, 2, 2), ("z", "y", "xl", "xh", "c"))
    small_t, large_t = cross_strips()
    along_t = along_table()
    pair = [(0, 1), (1, 0)]

    def swap(message):
        return lax.all_to_all(message, ("y", "z", "xl"), split_axis=0, concat_axis=0, tiled=True)

    def shards(moments):
        grid = moments.shape
        own = moments.reshape(ROWS * PLANES, LANES)
        far_a = lax.ppermute(own[:256], "xh", pair)
        near = lax.ppermute(own, "c", pair)
        home = swap(pack(moments.reshape(ROWS, PLANES, LANES)).reshape(64, 9, 4, 128))
        home, far_a, near = lax.optimization_barrier((home, far_a, near))
        far_b = lax.ppermute(own[256:], "xh", pair)
        back = swap(cross(jnp.asarray(small_t), jnp.asarray(large_t), home).reshape(64, 72, 128))
        far_near_a = lax.ppermute(far_a, "c", pair)
        far_near_b = lax.ppermute(far_b, "c", pair)
        core = lax.axis_index("c").reshape(1)
        first_z, second_z = along(
            core, jnp.asarray(along_t), own, near, far_a, far_b, far_near_a, far_near_b
        )
        first_z, second_z, back = lax.optimization_barrier((first_z, second_z, back))
        first, second = unpack(back.reshape(4608, 128))
        return (
            first.reshape(grid),
            second.reshape(grid),
            first_z.reshape(grid),
            second_z.reshape(grid),
        )

    spec = P(("z", "y", "xl"), None, None, ("xh", "c"))
    return jax.shard_map(
        shards, mesh=fine, in_specs=(spec,), out_specs=(spec,) * 4, check_vma=False
    )
```

```python
import math

import jax
import jax.numpy as jnp
import ml_dtypes
import numpy as np
from jax import lax
from jax.experimental import pallas as pl
from jax.experimental.pallas import tpu as pltpu
from jax.sharding import Mesh
from jax.sharding import PartitionSpec as P

COUNT = 1536
HALF = COUNT // 2
QUARTER = COUNT // 4
ROWS = 24
LANES = 384
PLANES = 32
F32 = jnp.float32
BF16 = jnp.bfloat16


def kernels():
    k = np.arange(COUNT, dtype=np.float64)
    sign = np.where(np.arange(COUNT) % 2 == 0, 1.0, -1.0)
    angle = math.pi * np.where(k == 0, 1.0, k) / COUNT
    first = np.where(k == 0, 0.0, math.pi / COUNT * sign / np.tan(angle))
    second = np.where(
        k == 0,
        -math.pi**2 / 3 - (2 * math.pi / COUNT) ** 2 / 6,
        -sign * (2 * math.pi**2 / COUNT**2) / np.sin(angle) ** 2,
    )
    return first, second


def halves(table):
    high = table.astype(ml_dtypes.bfloat16)
    low = (table - high.astype(np.float64)).astype(ml_dtypes.bfloat16)
    return np.stack([high, low])


def cross_strips():
    def strip(block, value):
        gap = 2 * block + np.arange(block)[:, None] - np.arange(5 * block)[None, :]
        return halves(np.stack([value(d, gap) for d in kernels()]))

    def plus(d, gap):
        return (d[gap % COUNT] + d[(gap + HALF) % COUNT]) / 2

    both = strip(128, lambda d, gap: (plus(d, gap) + plus(d, gap + QUARTER)) / 2)
    cross = strip(128, lambda d, gap: (plus(d, gap) - plus(d, gap + QUARTER)) / 2)
    minus = strip(256, lambda d, gap: (d[gap % COUNT] - d[(gap + HALF) % COUNT]) / 2)
    return np.stack([both, cross]), minus


def along_table():
    cell = np.arange(LANES)
    blocks = [
        np.concatenate(
            [d[(cell[None, :] - cell[:, None] - LANES * r) % COUNT] for d in kernels()], axis=1
        )
        for r in range(4)
    ]
    return halves(np.stack(blocks))


def split(value):
    high = value.astype(BF16)
    return high, (value - high.astype(F32)).astype(BF16)


def three(left_high, left_low, right_high, right_low):
    total = jnp.dot(left_high, right_high, preferred_element_type=F32)
    total = total + jnp.dot(left_high, right_low, preferred_element_type=F32)
    return total + jnp.dot(left_low, right_high, preferred_element_type=F32)


def low_lanes(shape):
    return lax.broadcasted_iota(jnp.int32, shape, len(shape) - 1) < 64


def pack_kernel(x_hbm, msg_hbm, x_ref, msg_ref, in_sems, out_sems):
    gets = [
        pltpu.make_async_copy(x_hbm.at[:, 8 * g : 8 * g + 8], x_ref.at[g], in_sems.at[g])
        for g in range(4)
    ]
    puts = [
        pltpu.make_async_copy(msg_ref.at[g], msg_hbm.at[576 * g : 576 * g + 576], out_sems.at[g])
        for g in range(4)
    ]
    near = low_lanes((8, 128))
    for get in gets:
        get.start()
    for g in range(4):
        gets[g].wait()
        for i in range(ROWS):
            for low in range(2):
                at = pl.ds(36 * low + i, 8, stride=72)
                msg_ref[g, at, :] = x_ref[g, i, :, 128 * low : 128 * low + 128]
        for i in range(12):
            top, bottom = x_ref[g, i, :, 256:384], x_ref[g, i + 12, :, 256:384]
            lower = jnp.where(near, top, pltpu.roll(bottom, 64, 1))
            upper = jnp.where(near, pltpu.roll(top, 64, 1), bottom)
            msg_ref[g, pl.ds(24 + i, 8, stride=72), :] = lower
            msg_ref[g, pl.ds(60 + i, 8, stride=72), :] = upper
        puts[g].start()
    for put in puts:
        put.wait()


def pack(block):
    return pl.pallas_call(
        pack_kernel,
        in_specs=[pl.BlockSpec(memory_space=pltpu.HBM)],
        out_specs=pl.BlockSpec(memory_space=pltpu.HBM),
        out_shape=jax.ShapeDtypeStruct((2304, 128), F32),
        scratch_shapes=[
            pltpu.VMEM((4, ROWS, 8, LANES), F32),
            pltpu.VMEM((4, 576, 128), F32),
            pltpu.SemaphoreType.DMA((4,)),
            pltpu.SemaphoreType.DMA((4,)),
        ],
        compiler_params=pltpu.CompilerParams(vmem_limit_bytes=56 * 2**20),
    )(block)


def unpack_kernel(msg_ref, first_hbm, second_hbm, out_ref, sems):
    near = low_lanes((8, 128))
    puts = []
    for g in range(4):
        base = 1152 * g
        for d, (out_hbm, full, part) in enumerate(((first_hbm, 0, 24), (second_hbm, 48, 36))):
            for i in range(ROWS):
                for low in range(2):
                    at = pl.ds(base + 72 * low + full + i, 8, stride=144)
                    out_ref[d, g, i, :, 128 * low : 128 * low + 128] = msg_ref[at, :]
            for i in range(12):
                lower = msg_ref[pl.ds(base + part + i, 8, stride=144), :]
                upper = msg_ref[pl.ds(base + 72 + part + i, 8, stride=144), :]
                out_ref[d, g, i, :, 256:384] = jnp.where(near, lower, pltpu.roll(upper, 64, 1))
                out_ref[d, g, i + 12, :, 256:384] = jnp.where(
                    near, pltpu.roll(lower, 64, 1), upper
                )
            put = pltpu.make_async_copy(
                out_ref.at[d, g], out_hbm.at[:, 8 * g : 8 * g + 8], sems.at[2 * g + d]
            )
            put.start()
            puts.append(put)
    for put in puts:
        put.wait()


def unpack(message):
    out = jax.ShapeDtypeStruct((ROWS, PLANES, LANES), F32)
    return pl.pallas_call(
        unpack_kernel,
        in_specs=[pl.BlockSpec(memory_space=pltpu.VMEM)],
        out_specs=[pl.BlockSpec(memory_space=pltpu.HBM)] * 2,
        out_shape=(out, out),
        scratch_shapes=[
            pltpu.VMEM((2, 4, ROWS, 8, LANES), F32),
            pltpu.SemaphoreType.DMA((8,)),
        ],
        compiler_params=pltpu.CompilerParams(vmem_limit_bytes=16 * 2**20),
    )(message)


def cross_kernel(
    small_hbm,
    large_hbm,
    msg_hbm,
    out_hbm,
    small_strip,
    large_strip,
    small,
    msg,
    out,
    line,
    got_small,
    got_large,
    in_sems,
    table_sems,
    out_sems,
):
    gets = [
        pltpu.make_async_copy(msg_hbm.at[:, c], msg.at[c], in_sems.at[c]) for c in range(4)
    ]
    strips = [
        pltpu.make_async_copy(small_hbm, small_strip, table_sems.at[0]),
        pltpu.make_async_copy(large_hbm, large_strip, table_sems.at[1]),
    ]
    puts = [pltpu.make_async_copy(out.at[z], out_hbm.at[z], out_sems.at[z]) for z in range(8)]
    for copy in gets + strips:
        copy.start()

    for c in range(4):
        gets[c].wait()
        for y in range(4):
            at = 48 * (4 * c + y)
            top, bottom = msg[c, 0, y], msg[c, 1, y]
            for k, value in enumerate((top + bottom, top - bottom)):
                line[k, at : at + 24, 0:128] = value[0:24]
                line[k, at + 24 : at + 48, 0:128] = value[36:60]
                even, odd = value[24:36], value[60:72]
                parts = [even, pltpu.roll(even, 64, 1), odd, pltpu.roll(odd, 64, 1)]
                line[k, at : at + 48, 128:256] = jnp.concatenate(parts, axis=0)

    for copy in strips:
        copy.wait()
    for h in range(2):
        for d in range(2):
            for i in range(3):
                rows = slice(QUARTER * d + 128 * i, QUARTER * d + 128 * i + 128)
                lanes = slice(128 * (2 - i), 128 * (2 - i) + QUARTER)
                for k in range(2):
                    small[k, h, rows, :] = small_strip[k, h, d, :, lanes]
    head, tail = line[0, :QUARTER, :], line[0, QUARTER:, :]
    whole = head + tail
    whole = whole - jnp.sum(whole, axis=0, keepdims=True) * (1.0 / QUARTER)
    for k, value in enumerate((whole, head - tail)):
        high, low = split(value)
        got_small[k] = three(small[k, 0], small[k, 1], high, low)

    high, low = split(line[1])
    near = low_lanes((12, 128))

    def products(i):
        for d in range(2):
            lanes = slice(256 * (2 - i), 256 * (2 - i) + HALF)
            left = large_strip[0, d, :, lanes], large_strip[1, d, :, lanes]
            got_large[HALF * d + 256 * i : HALF * d + 256 * i + 256, :] = three(*left, high, low)

    def close(c):
        for y in range(4):
            for part_of in range(2):
                at = 48 * (4 * c + y) + ROWS * part_of
                for d, (full, part) in enumerate(((0, 24), (48, 36))):
                    minus = got_large[HALF * d + at : HALF * d + at + ROWS, :]
                    place = QUARTER * d + at % QUARTER
                    one = got_small[0, place : place + ROWS, :]
                    two = got_small[1, place : place + ROWS, :]
                    plus = one + two if at < QUARTER else one - two
                    for z, value in ((c, plus + minus), (c + 4, plus - minus)):
                        out[z, y, part_of, full : full + 24] = value[:, 0:128]
                        top, bottom = value[:12, 128:256], value[12:, 128:256]
                        out[z, y, part_of, part : part + 12] = jnp.where(
                            near, top, pltpu.roll(bottom, 64, 1)
                        )
        puts[c].start()
        puts[c + 4].start()

    products(0)
    products(1)
    close(0)
    products(2)
    close(1)
    close(2)
    close(3)
    for put in puts:
        put.wait()


def cross(small, large, message):
    return pl.pallas_call(
        cross_kernel,
        out_shape=jax.ShapeDtypeStruct((8, 4, 2, 72, 128), F32),
        in_specs=[
            pl.BlockSpec(memory_space=pltpu.HBM),
            pl.BlockSpec(memory_space=pltpu.HBM),
            pl.BlockSpec(memory_space=pl.ANY),
        ],
        out_specs=pl.BlockSpec(memory_space=pltpu.HBM),
        scratch_shapes=[
            pltpu.VMEM(small.shape, BF16),
            pltpu.VMEM(large.shape, BF16),
            pltpu.VMEM((2, 2, HALF, QUARTER), BF16),
            pltpu.VMEM((4, 2, 4, 72, 128), F32),
            pltpu.VMEM((8, 4, 2, 72, 128), F32),
            pltpu.VMEM((2, HALF, 256), F32),
            pltpu.VMEM((2, HALF, 256), F32),
            pltpu.VMEM((COUNT, 256), F32),
            pltpu.SemaphoreType.DMA((4,)),
            pltpu.SemaphoreType.DMA((2,)),
            pltpu.SemaphoreType.DMA((8,)),
        ],
        compiler_params=pltpu.CompilerParams(vmem_limit_bytes=60 * 2**20),
        cost_estimate=pl.CostEstimate(
            flops=3 * 2 * 3 * HALF * HALF * 256, bytes_accessed=12 * 2**20, transcendentals=0
        ),
    )(small, large, message.reshape(2, 4, 4, 72, 128))


def along_kernel(
    core_ref, table_ref, own, near, far_a, far_b, far_near_a, far_near_b, first_ref, second_ref
):
    core = core_ref[0]
    early = pl.program_id(0) == 0
    far = jnp.where(early, far_a[...], far_b[...])
    far_near = jnp.where(early, far_near_a[...], far_near_b[...])
    total = jnp.zeros((256, 2 * LANES), F32)
    pairs = ((own[...], 0), (near[...], 1 + 2 * core), (far, 2), (far_near, 3 - 2 * core))
    level = jnp.sum(own[...], axis=1, keepdims=True) * (1.0 / LANES)
    for block, r in pairs:
        high, low = split(block - level)
        total = total + three(high, low, table_ref[0, r], table_ref[1, r])
    first_ref[...] = total[:, :LANES]
    second_ref[...] = total[:, LANES:]


def along(core, table, *blocks):
    out = jax.ShapeDtypeStruct((ROWS * PLANES, LANES), F32)
    lines = pl.BlockSpec((256, LANES), lambda i, core: (i, 0))
    early = pl.BlockSpec((256, LANES), lambda i, core: (0, 0))
    late = pl.BlockSpec((256, LANES), lambda i, core: (jnp.maximum(i, 1) - 1, 0))
    return pl.pallas_call(
        along_kernel,
        grid_spec=pltpu.PrefetchScalarGridSpec(
            num_scalar_prefetch=1,
            grid=(3,),
            in_specs=[pl.BlockSpec((2, 4, LANES, 2 * LANES), lambda i, core: (0, 0, 0, 0))]
            + [lines, lines, early, late, early, late],
            out_specs=[lines] * 2,
        ),
        out_shape=(out, out),
        compiler_params=pltpu.CompilerParams(vmem_limit_bytes=24 * 2**20),
        cost_estimate=pl.CostEstimate(
            flops=2 * 3 * 768 * COUNT * 768, bytes_accessed=16 * 2**20, transcendentals=0
        ),
    )(core, table, *blocks)


def solution(mesh):
    fine = Mesh(mesh.devices.reshape(8, 4, 2, 2, 2), ("z", "y", "xl", "xh", "c"))
    small_t, large_t = cross_strips()
    along_t = along_table()
    pair = [(0, 1), (1, 0)]

    def swap(message):
        return lax.all_to_all(message, ("z", "y", "xl"), split_axis=0, concat_axis=0, tiled=True)

    def shards(moments):
        grid = moments.shape
        own = moments.reshape(ROWS * PLANES, LANES)
        far_a = lax.ppermute(own[:256], "xh", pair)
        near = lax.ppermute(own, "c", pair)
        home = swap(pack(moments.reshape(ROWS, PLANES, LANES)).reshape(64, 9, 4, 128))
        home, far_a, near = lax.optimization_barrier((home, far_a, near))
        far_b = lax.ppermute(own[256:], "xh", pair)
        back = swap(cross(jnp.asarray(small_t), jnp.asarray(large_t), home).reshape(64, 72, 128))
        far_near_a = lax.ppermute(far_a, "c", pair)
        far_near_b = lax.ppermute(far_b, "c", pair)
        core = lax.axis_index("c").reshape(1)
        first_z, second_z = along(
            core, jnp.asarray(along_t), own, near, far_a, far_b, far_near_a, far_near_b
        )
        first_z, second_z, back = lax.optimization_barrier((first_z, second_z, back))
        first, second = unpack(back.reshape(4608, 128))
        return (
            first.reshape(grid),
            second.reshape(grid),
            first_z.reshape(grid),
            second_z.reshape(grid),
        )

    spec = P(("z", "y", "xl"), None, None, ("xh", "c"))
    return jax.shard_map(
        shards, mesh=fine, in_specs=(spec,), out_specs=(spec,) * 4, check_vma=False
    )
```

```python
import math

import jax
import jax.numpy as jnp
import ml_dtypes
import numpy as np
from jax import lax
from jax.experimental import pallas as pl
from jax.experimental.pallas import tpu as pltpu
from jax.sharding import Mesh
from jax.sharding import PartitionSpec as P

COUNT = 1536
HALF = COUNT // 2
QUARTER = COUNT // 4
ROWS = 24
LANES = 384
PLANES = 32
F32 = jnp.float32
BF16 = jnp.bfloat16


def kernels():
    k = np.arange(COUNT, dtype=np.float64)
    sign = np.where(np.arange(COUNT) % 2 == 0, 1.0, -1.0)
    angle = math.pi * np.where(k == 0, 1.0, k) / COUNT
    first = np.where(k == 0, 0.0, math.pi / COUNT * sign / np.tan(angle))
    second = np.where(
        k == 0,
        -math.pi**2 / 3 - (2 * math.pi / COUNT) ** 2 / 6,
        -sign * (2 * math.pi**2 / COUNT**2) / np.sin(angle) ** 2,
    )
    return first, second


def halves(table):
    high = table.astype(ml_dtypes.bfloat16)
    low = (table - high.astype(np.float64)).astype(ml_dtypes.bfloat16)
    return np.stack([high, low])


def cross_strips():
    def strip(block, value):
        gap = 2 * block + np.arange(block)[:, None] - np.arange(5 * block)[None, :]
        return halves(np.stack([value(d, gap) for d in kernels()]))

    def plus(d, gap):
        return (d[gap % COUNT] + d[(gap + HALF) % COUNT]) / 2

    both = strip(128, lambda d, gap: (plus(d, gap) + plus(d, gap + QUARTER)) / 2)
    cross = strip(128, lambda d, gap: (plus(d, gap) - plus(d, gap + QUARTER)) / 2)
    minus = strip(256, lambda d, gap: (d[gap % COUNT] - d[(gap + HALF) % COUNT]) / 2)
    return np.stack([both, cross]), minus


def along_table():
    cell = np.arange(LANES)
    blocks = [
        np.concatenate(
            [d[(cell[None, :] - cell[:, None] - LANES * r) % COUNT] for d in kernels()], axis=1
        )
        for r in range(4)
    ]
    return halves(np.stack(blocks))


def split(value):
    high = value.astype(BF16)
    return high, (value - high.astype(F32)).astype(BF16)


def three(left_high, left_low, right_high, right_low):
    total = jnp.dot(left_high, right_high, preferred_element_type=F32)
    total = total + jnp.dot(left_high, right_low, preferred_element_type=F32)
    return total + jnp.dot(left_low, right_high, preferred_element_type=F32)


def low_lanes(shape):
    return lax.broadcasted_iota(jnp.int32, shape, len(shape) - 1) < 64


def pack_kernel(x_hbm, msg_hbm, x_ref, msg_ref, in_sems, out_sems):
    gets = [
        pltpu.make_async_copy(x_hbm.at[:, 8 * g : 8 * g + 8], x_ref.at[g], in_sems.at[g])
        for g in range(4)
    ]
    puts = [
        pltpu.make_async_copy(msg_ref.at[g], msg_hbm.at[576 * g : 576 * g + 576], out_sems.at[g])
        for g in range(4)
    ]
    near = low_lanes((8, 128))
    for get in gets:
        get.start()
    for g in range(4):
        gets[g].wait()
        for i in range(ROWS):
            for low in range(2):
                at = pl.ds(36 * low + i, 8, stride=72)
                msg_ref[g, at, :] = x_ref[g, i, :, 128 * low : 128 * low + 128]
        for i in range(12):
            top, bottom = x_ref[g, i, :, 256:384], x_ref[g, i + 12, :, 256:384]
            lower = jnp.where(near, top, pltpu.roll(bottom, 64, 1))
            upper = jnp.where(near, pltpu.roll(top, 64, 1), bottom)
            msg_ref[g, pl.ds(24 + i, 8, stride=72), :] = lower
            msg_ref[g, pl.ds(60 + i, 8, stride=72), :] = upper
        puts[g].start()
    for put in puts:
        put.wait()


def pack(block):
    return pl.pallas_call(
        pack_kernel,
        in_specs=[pl.BlockSpec(memory_space=pltpu.HBM)],
        out_specs=pl.BlockSpec(memory_space=pltpu.HBM),
        out_shape=jax.ShapeDtypeStruct((2304, 128), F32),
        scratch_shapes=[
            pltpu.VMEM((4, ROWS, 8, LANES), F32),
            pltpu.VMEM((4, 576, 128), F32),
            pltpu.SemaphoreType.DMA((4,)),
            pltpu.SemaphoreType.DMA((4,)),
        ],
        compiler_params=pltpu.CompilerParams(vmem_limit_bytes=56 * 2**20),
    )(block)


def unpack_kernel(msg_ref, first_hbm, second_hbm, out_ref, sems):
    near = low_lanes((8, 128))
    puts = []
    for g in range(4):
        base = 1152 * g
        for d, (out_hbm, full, part) in enumerate(((first_hbm, 0, 24), (second_hbm, 48, 36))):
            for i in range(ROWS):
                for low in range(2):
                    at = pl.ds(base + 72 * low + full + i, 8, stride=144)
                    out_ref[d, g, i, :, 128 * low : 128 * low + 128] = msg_ref[at, :]
            for i in range(12):
                lower = msg_ref[pl.ds(base + part + i, 8, stride=144), :]
                upper = msg_ref[pl.ds(base + 72 + part + i, 8, stride=144), :]
                out_ref[d, g, i, :, 256:384] = jnp.where(near, lower, pltpu.roll(upper, 64, 1))
                out_ref[d, g, i + 12, :, 256:384] = jnp.where(
                    near, pltpu.roll(lower, 64, 1), upper
                )
            put = pltpu.make_async_copy(
                out_ref.at[d, g], out_hbm.at[:, 8 * g : 8 * g + 8], sems.at[2 * g + d]
            )
            put.start()
            puts.append(put)
    for put in puts:
        put.wait()


def unpack(message):
    out = jax.ShapeDtypeStruct((ROWS, PLANES, LANES), F32)
    return pl.pallas_call(
        unpack_kernel,
        in_specs=[pl.BlockSpec(memory_space=pltpu.VMEM)],
        out_specs=[pl.BlockSpec(memory_space=pltpu.HBM)] * 2,
        out_shape=(out, out),
        scratch_shapes=[
            pltpu.VMEM((2, 4, ROWS, 8, LANES), F32),
            pltpu.SemaphoreType.DMA((8,)),
        ],
        compiler_params=pltpu.CompilerParams(vmem_limit_bytes=16 * 2**20),
    )(message)


def cross_kernel(
    small_hbm,
    large_hbm,
    msg_hbm,
    out_hbm,
    small_strip,
    large_strip,
    small,
    msg,
    out,
    line,
    got_small,
    got_large,
    in_sems,
    table_sems,
    out_sems,
):
    gets = [
        pltpu.make_async_copy(msg_hbm.at[:, c], msg.at[c], in_sems.at[c]) for c in range(4)
    ]
    strips = [
        pltpu.make_async_copy(small_hbm, small_strip, table_sems.at[0]),
        pltpu.make_async_copy(large_hbm, large_strip, table_sems.at[1]),
    ]
    puts = [pltpu.make_async_copy(out.at[z], out_hbm.at[z], out_sems.at[z]) for z in range(8)]
    for copy in gets + strips:
        copy.start()

    for c in range(4):
        gets[c].wait()
        for y in range(4):
            at = 48 * (4 * c + y)
            top, bottom = msg[c, 0, y], msg[c, 1, y]
            for k, value in enumerate((top + bottom, top - bottom)):
                line[k, at : at + 24, 0:128] = value[0:24]
                line[k, at + 24 : at + 48, 0:128] = value[36:60]
                even, odd = value[24:36], value[60:72]
                parts = [even, pltpu.roll(even, 64, 1), odd, pltpu.roll(odd, 64, 1)]
                line[k, at : at + 48, 128:256] = jnp.concatenate(parts, axis=0)

    for copy in strips:
        copy.wait()
    for h in range(2):
        for d in range(2):
            for i in range(3):
                rows = slice(QUARTER * d + 128 * i, QUARTER * d + 128 * i + 128)
                lanes = slice(128 * (2 - i), 128 * (2 - i) + QUARTER)
                for k in range(2):
                    small[k, h, rows, :] = small_strip[k, h, d, :, lanes]
    head, tail = line[0, :QUARTER, :], line[0, QUARTER:, :]
    whole = head + tail
    whole = whole - jnp.sum(whole, axis=0, keepdims=True) * (1.0 / QUARTER)
    for k, value in enumerate((whole, head - tail)):
        high, low = split(value)
        got_small[k] = three(small[k, 0], small[k, 1], high, low)

    high, low = split(line[1])
    near = low_lanes((12, 128))

    def products(i):
        for d in range(2):
            lanes = slice(256 * (2 - i), 256 * (2 - i) + HALF)
            left = large_strip[0, d, :, lanes], large_strip[1, d, :, lanes]
            got_large[HALF * d + 256 * i : HALF * d + 256 * i + 256, :] = three(*left, high, low)

    def close(c):
        for y in range(4):
            for part_of in range(2):
                at = 48 * (4 * c + y) + ROWS * part_of
                for d, (full, part) in enumerate(((0, 24), (48, 36))):
                    minus = got_large[HALF * d + at : HALF * d + at + ROWS, :]
                    place = QUARTER * d + at % QUARTER
                    one = got_small[0, place : place + ROWS, :]
                    two = got_small[1, place : place + ROWS, :]
                    plus = one + two if at < QUARTER else one - two
                    for z, value in ((c, plus + minus), (c + 4, plus - minus)):
                        out[z, y, part_of, full : full + 24] = value[:, 0:128]
                        top, bottom = value[:12, 128:256], value[12:, 128:256]
                        out[z, y, part_of, part : part + 12] = jnp.where(
                            near, top, pltpu.roll(bottom, 64, 1)
                        )
        puts[c].start()
        puts[c + 4].start()

    products(0)
    products(1)
    close(0)
    products(2)
    close(1)
    close(2)
    close(3)
    for put in puts:
        put.wait()


def cross(small, large, message):
    return pl.pallas_call(
        cross_kernel,
        out_shape=jax.ShapeDtypeStruct((8, 4, 2, 72, 128), F32),
        in_specs=[
            pl.BlockSpec(memory_space=pltpu.HBM),
            pl.BlockSpec(memory_space=pltpu.HBM),
            pl.BlockSpec(memory_space=pl.ANY),
        ],
        out_specs=pl.BlockSpec(memory_space=pltpu.HBM),
        scratch_shapes=[
            pltpu.VMEM(small.shape, BF16),
            pltpu.VMEM(large.shape, BF16),
            pltpu.VMEM((2, 2, HALF, QUARTER), BF16),
            pltpu.VMEM((4, 2, 4, 72, 128), F32),
            pltpu.VMEM((8, 4, 2, 72, 128), F32),
            pltpu.VMEM((2, HALF, 256), F32),
            pltpu.VMEM((2, HALF, 256), F32),
            pltpu.VMEM((COUNT, 256), F32),
            pltpu.SemaphoreType.DMA((4,)),
            pltpu.SemaphoreType.DMA((2,)),
            pltpu.SemaphoreType.DMA((8,)),
        ],
        compiler_params=pltpu.CompilerParams(vmem_limit_bytes=60 * 2**20),
        cost_estimate=pl.CostEstimate(
            flops=3 * 2 * 3 * HALF * HALF * 256, bytes_accessed=12 * 2**20, transcendentals=0
        ),
    )(small, large, message.reshape(2, 4, 4, 72, 128))


def add_lines(total, table_ref, pairs, level):
    for block, r in pairs:
        high, low = split(block - level)
        total = total + three(high, low, table_ref[0, r], table_ref[1, r])
    return total


def line_level(own):
    return jnp.sum(own[...], axis=1, keepdims=True) * (1.0 / LANES)


def close_kernel(core_ref, table_ref, own, near, out_ref):
    pairs = ((own[...], 0), (near[...], 1 + 2 * core_ref[0]))
    total = jnp.zeros((256, 2 * LANES), F32)
    out_ref[...] = add_lines(total, table_ref, pairs, line_level(own))


def far_kernel(
    core_ref, table_ref, own, part, far_a, far_b, far_near_a, far_near_b, first_ref, second_ref
):
    early = pl.program_id(0) == 0
    far = jnp.where(early, far_a[...], far_b[...])
    far_near = jnp.where(early, far_near_a[...], far_near_b[...])
    pairs = ((far, 2), (far_near, 3 - 2 * core_ref[0]))
    total = add_lines(part[...], table_ref, pairs, line_level(own))
    first_ref[...] = total[:, :LANES]
    second_ref[...] = total[:, LANES:]


LINES = pl.BlockSpec((256, LANES), lambda i, core: (i, 0))
BOTH = pl.BlockSpec((256, 2 * LANES), lambda i, core: (i, 0))


def along(kernel, ins, outs, shapes):
    return pl.pallas_call(
        kernel,
        grid_spec=pltpu.PrefetchScalarGridSpec(
            num_scalar_prefetch=1,
            grid=(3,),
            in_specs=[pl.BlockSpec((2, 4, LANES, 2 * LANES), lambda i, core: (0, 0, 0, 0))] + ins,
            out_specs=outs,
        ),
        out_shape=shapes,
        compiler_params=pltpu.CompilerParams(vmem_limit_bytes=24 * 2**20),
        cost_estimate=pl.CostEstimate(
            flops=3 * 768 * COUNT * 768, bytes_accessed=12 * 2**20, transcendentals=0
        ),
    )


def along_close(*args):
    shape = jax.ShapeDtypeStruct((ROWS * PLANES, 2 * LANES), F32)
    return along(close_kernel, [LINES, LINES], BOTH, shape)(*args)


def along_far(*args):
    out = jax.ShapeDtypeStruct((ROWS * PLANES, LANES), F32)
    early = pl.BlockSpec((256, LANES), lambda i, core: (0, 0))
    late = pl.BlockSpec((256, LANES), lambda i, core: (jnp.maximum(i, 1) - 1, 0))
    ins = [LINES, BOTH, early, late, early, late]
    return along(far_kernel, ins, [LINES] * 2, (out, out))(*args)


def solution(mesh):
    fine = Mesh(mesh.devices.reshape(8, 4, 2, 2, 2), ("z", "y", "xl", "xh", "c"))
    small_t, large_t = cross_strips()
    along_t = along_table()
    pair = [(0, 1), (1, 0)]

    def swap(message):
        return lax.all_to_all(message, ("z", "y", "xl"), split_axis=0, concat_axis=0, tiled=True)

    def shards(moments):
        grid = moments.shape
        own = moments.reshape(ROWS * PLANES, LANES)
        far_a = lax.ppermute(own[:256], "xh", pair)
        near = lax.ppermute(own, "c", pair)
        home = swap(pack(moments.reshape(ROWS, PLANES, LANES)).reshape(64, 9, 4, 128))
        home, far_a, near = lax.optimization_barrier((home, far_a, near))
        far_b = lax.ppermute(own[256:], "xh", pair)
        back = swap(cross(jnp.asarray(small_t), jnp.asarray(large_t), home).reshape(64, 72, 128))
        far_near_a = lax.ppermute(far_a, "c", pair)
        far_near_b = lax.ppermute(far_b, "c", pair)
        core = lax.axis_index("c").reshape(1)
        table = jnp.asarray(along_t)
        part = along_close(core, table, own, near)
        first_z, second_z = along_far(
            core, table, own, part, far_a, far_b, far_near_a, far_near_b
        )
        first_z, second_z, back = lax.optimization_barrier((first_z, second_z, back))
        first, second = unpack(back.reshape(4608, 128))
        return (
            first.reshape(grid),
            second.reshape(grid),
            first_z.reshape(grid),
            second_z.reshape(grid),
        )

    spec = P(("z", "y", "xl"), None, None, ("xh", "c"))
    return jax.shard_map(
        shards, mesh=fine, in_specs=(spec,), out_specs=(spec,) * 4, check_vma=False
    )
```

```python
import math

import jax
import jax.numpy as jnp
import ml_dtypes
import numpy as np
from jax import lax
from jax.experimental import pallas as pl
from jax.experimental.pallas import tpu as pltpu
from jax.sharding import Mesh
from jax.sharding import PartitionSpec as P

COUNT = 1536
HALF = COUNT // 2
QUARTER = COUNT // 4
ROWS = 24
LANES = 384
PLANES = 32
F32 = jnp.float32
BF16 = jnp.bfloat16


def kernels():
    k = np.arange(COUNT, dtype=np.float64)
    sign = np.where(np.arange(COUNT) % 2 == 0, 1.0, -1.0)
    angle = math.pi * np.where(k == 0, 1.0, k) / COUNT
    first = np.where(k == 0, 0.0, math.pi / COUNT * sign / np.tan(angle))
    second = np.where(
        k == 0,
        -math.pi**2 / 3 - (2 * math.pi / COUNT) ** 2 / 6,
        -sign * (2 * math.pi**2 / COUNT**2) / np.sin(angle) ** 2,
    )
    return first, second


def halves(table):
    high = table.astype(ml_dtypes.bfloat16)
    low = (table - high.astype(np.float64)).astype(ml_dtypes.bfloat16)
    return np.stack([high, low])


def cross_strips():
    def strip(block, value):
        gap = 2 * block + np.arange(block)[:, None] - np.arange(5 * block)[None, :]
        return halves(np.stack([value(d, gap) for d in kernels()]))

    def plus(d, gap):
        return (d[gap % COUNT] + d[(gap + HALF) % COUNT]) / 2

    both = strip(128, lambda d, gap: (plus(d, gap) + plus(d, gap + QUARTER)) / 2)
    cross = strip(128, lambda d, gap: (plus(d, gap) - plus(d, gap + QUARTER)) / 2)
    minus = strip(256, lambda d, gap: (d[gap % COUNT] - d[(gap + HALF) % COUNT]) / 2)
    return np.stack([both, cross]), minus


def along_table():
    cell = np.arange(LANES)
    blocks = [
        np.concatenate(
            [d[(cell[None, :] - cell[:, None] - LANES * r) % COUNT] for d in kernels()], axis=1
        )
        for r in range(4)
    ]
    return halves(np.stack(blocks))


def split(value):
    high = value.astype(BF16)
    return high, (value - high.astype(F32)).astype(BF16)


def three(left_high, left_low, right_high, right_low):
    total = jnp.dot(left_high, right_high, preferred_element_type=F32)
    total = total + jnp.dot(left_high, right_low, preferred_element_type=F32)
    return total + jnp.dot(left_low, right_high, preferred_element_type=F32)


def low_lanes(shape):
    return lax.broadcasted_iota(jnp.int32, shape, len(shape) - 1) < 64


def pack_kernel(x_hbm, msg_hbm, x_ref, msg_ref, in_sems, out_sems):
    gets = [
        pltpu.make_async_copy(x_hbm.at[:, 8 * g : 8 * g + 8], x_ref.at[g], in_sems.at[g])
        for g in range(4)
    ]
    puts = [
        pltpu.make_async_copy(msg_ref.at[g], msg_hbm.at[576 * g : 576 * g + 576], out_sems.at[g])
        for g in range(4)
    ]
    near = low_lanes((8, 128))
    for get in gets:
        get.start()
    for g in range(4):
        gets[g].wait()
        for i in range(ROWS):
            for low in range(2):
                at = pl.ds(36 * low + i, 8, stride=72)
                msg_ref[g, at, :] = x_ref[g, i, :, 128 * low : 128 * low + 128]
        for i in range(12):
            top, bottom = x_ref[g, i, :, 256:384], x_ref[g, i + 12, :, 256:384]
            lower = jnp.where(near, top, pltpu.roll(bottom, 64, 1))
            upper = jnp.where(near, pltpu.roll(top, 64, 1), bottom)
            msg_ref[g, pl.ds(24 + i, 8, stride=72), :] = lower
            msg_ref[g, pl.ds(60 + i, 8, stride=72), :] = upper
        puts[g].start()
    for put in puts:
        put.wait()


def pack(block):
    return pl.pallas_call(
        pack_kernel,
        in_specs=[pl.BlockSpec(memory_space=pltpu.HBM)],
        out_specs=pl.BlockSpec(memory_space=pltpu.HBM),
        out_shape=jax.ShapeDtypeStruct((2304, 128), F32),
        scratch_shapes=[
            pltpu.VMEM((4, ROWS, 8, LANES), F32),
            pltpu.VMEM((4, 576, 128), F32),
            pltpu.SemaphoreType.DMA((4,)),
            pltpu.SemaphoreType.DMA((4,)),
        ],
        compiler_params=pltpu.CompilerParams(vmem_limit_bytes=56 * 2**20),
    )(block)


def unpack_kernel(msg_ref, first_hbm, second_hbm, out_ref, sems):
    near = low_lanes((8, 128))
    puts = []
    for g in range(4):
        base = 1152 * g
        for d, (out_hbm, full, part) in enumerate(((first_hbm, 0, 24), (second_hbm, 48, 36))):
            for i in range(ROWS):
                for low in range(2):
                    at = pl.ds(base + 72 * low + full + i, 8, stride=144)
                    out_ref[d, g, i, :, 128 * low : 128 * low + 128] = msg_ref[at, :]
            for i in range(12):
                lower = msg_ref[pl.ds(base + part + i, 8, stride=144), :]
                upper = msg_ref[pl.ds(base + 72 + part + i, 8, stride=144), :]
                out_ref[d, g, i, :, 256:384] = jnp.where(near, lower, pltpu.roll(upper, 64, 1))
                out_ref[d, g, i + 12, :, 256:384] = jnp.where(
                    near, pltpu.roll(lower, 64, 1), upper
                )
            put = pltpu.make_async_copy(
                out_ref.at[d, g], out_hbm.at[:, 8 * g : 8 * g + 8], sems.at[2 * g + d]
            )
            put.start()
            puts.append(put)
    for put in puts:
        put.wait()


def unpack(message):
    out = jax.ShapeDtypeStruct((ROWS, PLANES, LANES), F32)
    return pl.pallas_call(
        unpack_kernel,
        in_specs=[pl.BlockSpec(memory_space=pltpu.VMEM)],
        out_specs=[pl.BlockSpec(memory_space=pltpu.HBM)] * 2,
        out_shape=(out, out),
        scratch_shapes=[
            pltpu.VMEM((2, 4, ROWS, 8, LANES), F32),
            pltpu.SemaphoreType.DMA((8,)),
        ],
        compiler_params=pltpu.CompilerParams(vmem_limit_bytes=16 * 2**20),
    )(message)


def cross_kernel(
    small_hbm,
    large_hbm,
    msg_hbm,
    out_hbm,
    small_strip,
    large_strip,
    small,
    msg,
    out,
    line,
    got_small,
    got_large,
    in_sems,
    table_sems,
    out_sems,
):
    gets = [
        pltpu.make_async_copy(msg_hbm.at[:, c], msg.at[c], in_sems.at[c]) for c in range(4)
    ]
    strips = [
        pltpu.make_async_copy(small_hbm, small_strip, table_sems.at[0]),
        pltpu.make_async_copy(large_hbm, large_strip, table_sems.at[1]),
    ]
    puts = [pltpu.make_async_copy(out.at[z], out_hbm.at[z], out_sems.at[z]) for z in range(8)]
    for copy in gets + strips:
        copy.start()

    for c in range(4):
        gets[c].wait()
        for y in range(4):
            at = 48 * (4 * c + y)
            top, bottom = msg[c, 0, y], msg[c, 1, y]
            for k, value in enumerate((top + bottom, top - bottom)):
                line[k, at : at + 24, 0:128] = value[0:24]
                line[k, at + 24 : at + 48, 0:128] = value[36:60]
                even, odd = value[24:36], value[60:72]
                parts = [even, pltpu.roll(even, 64, 1), odd, pltpu.roll(odd, 64, 1)]
                line[k, at : at + 48, 128:256] = jnp.concatenate(parts, axis=0)

    for copy in strips:
        copy.wait()
    for h in range(2):
        for d in range(2):
            for i in range(3):
                rows = slice(QUARTER * d + 128 * i, QUARTER * d + 128 * i + 128)
                lanes = slice(128 * (2 - i), 128 * (2 - i) + QUARTER)
                for k in range(2):
                    small[k, h, rows, :] = small_strip[k, h, d, :, lanes]
    head, tail = line[0, :QUARTER, :], line[0, QUARTER:, :]
    whole = head + tail
    whole = whole - jnp.sum(whole, axis=0, keepdims=True) * (1.0 / QUARTER)
    for k, value in enumerate((whole, head - tail)):
        high, low = split(value)
        got_small[k] = three(small[k, 0], small[k, 1], high, low)

    high, low = split(line[1])
    near = low_lanes((12, 128))

    def products(i):
        for d in range(2):
            lanes = slice(256 * (2 - i), 256 * (2 - i) + HALF)
            left = large_strip[0, d, :, lanes], large_strip[1, d, :, lanes]
            got_large[HALF * d + 256 * i : HALF * d + 256 * i + 256, :] = three(*left, high, low)

    def close(c):
        for y in range(4):
            for part_of in range(2):
                at = 48 * (4 * c + y) + ROWS * part_of
                for d, (full, part) in enumerate(((0, 24), (48, 36))):
                    minus = got_large[HALF * d + at : HALF * d + at + ROWS, :]
                    place = QUARTER * d + at % QUARTER
                    one = got_small[0, place : place + ROWS, :]
                    two = got_small[1, place : place + ROWS, :]
                    plus = one + two if at < QUARTER else one - two
                    for z, value in ((c, plus + minus), (c + 4, plus - minus)):
                        out[z, y, part_of, full : full + 24] = value[:, 0:128]
                        top, bottom = value[:12, 128:256], value[12:, 128:256]
                        out[z, y, part_of, part : part + 12] = jnp.where(
                            near, top, pltpu.roll(bottom, 64, 1)
                        )
        puts[c].start()
        puts[c + 4].start()

    products(0)
    products(1)
    close(0)
    products(2)
    close(1)
    close(2)
    close(3)
    for put in puts:
        put.wait()


def cross(small, large, message):
    return pl.pallas_call(
        cross_kernel,
        out_shape=jax.ShapeDtypeStruct((8, 4, 2, 72, 128), F32),
        in_specs=[
            pl.BlockSpec(memory_space=pltpu.HBM),
            pl.BlockSpec(memory_space=pltpu.HBM),
            pl.BlockSpec(memory_space=pl.ANY),
        ],
        out_specs=pl.BlockSpec(memory_space=pltpu.HBM),
        scratch_shapes=[
            pltpu.VMEM(small.shape, BF16),
            pltpu.VMEM(large.shape, BF16),
            pltpu.VMEM((2, 2, HALF, QUARTER), BF16),
            pltpu.VMEM((4, 2, 4, 72, 128), F32),
            pltpu.VMEM((8, 4, 2, 72, 128), F32),
            pltpu.VMEM((2, HALF, 256), F32),
            pltpu.VMEM((2, HALF, 256), F32),
            pltpu.VMEM((COUNT, 256), F32),
            pltpu.SemaphoreType.DMA((4,)),
            pltpu.SemaphoreType.DMA((2,)),
            pltpu.SemaphoreType.DMA((8,)),
        ],
        compiler_params=pltpu.CompilerParams(vmem_limit_bytes=56 * 2**20),
        cost_estimate=pl.CostEstimate(
            flops=3 * 2 * 3 * HALF * HALF * 256, bytes_accessed=12 * 2**20, transcendentals=0
        ),
    )(small, large, message.reshape(2, 4, 4, 72, 128))


def add_lines(total, table_ref, pairs, level):
    for block, r in pairs:
        high, low = split(block - level)
        total = total + three(high, low, table_ref[0, r], table_ref[1, r])
    return total


def line_level(own):
    return jnp.sum(own[...], axis=1, keepdims=True) * (1.0 / LANES)


def close_kernel(core_ref, table_ref, own, near, out_ref):
    pairs = ((own[...], 0), (near[...], 1 + 2 * core_ref[0]))
    total = jnp.zeros((256, 2 * LANES), F32)
    out_ref[...] = add_lines(total, table_ref, pairs, line_level(own))


def far_kernel(
    core_ref, table_ref, own, part, far_a, far_b, far_near_a, far_near_b, first_ref, second_ref
):
    early = pl.program_id(0) == 0
    far = jnp.where(early, far_a[...], far_b[...])
    far_near = jnp.where(early, far_near_a[...], far_near_b[...])
    pairs = ((far, 2), (far_near, 3 - 2 * core_ref[0]))
    total = add_lines(part[...], table_ref, pairs, line_level(own))
    first_ref[...] = total[:, :LANES]
    second_ref[...] = total[:, LANES:]


LINES = pl.BlockSpec((256, LANES), lambda i, core: (i, 0))
BOTH = pl.BlockSpec((256, 2 * LANES), lambda i, core: (i, 0))


def along(kernel, ins, outs, shapes):
    return pl.pallas_call(
        kernel,
        grid_spec=pltpu.PrefetchScalarGridSpec(
            num_scalar_prefetch=1,
            grid=(3,),
            in_specs=[pl.BlockSpec((2, 4, LANES, 2 * LANES), lambda i, core: (0, 0, 0, 0))] + ins,
            out_specs=outs,
        ),
        out_shape=shapes,
        compiler_params=pltpu.CompilerParams(vmem_limit_bytes=24 * 2**20),
        cost_estimate=pl.CostEstimate(
            flops=3 * 768 * COUNT * 768, bytes_accessed=12 * 2**20, transcendentals=0
        ),
    )


def along_close(*args):
    shape = jax.ShapeDtypeStruct((ROWS * PLANES, 2 * LANES), F32)
    return along(close_kernel, [LINES, LINES], BOTH, shape)(*args)


def along_far(*args):
    out = jax.ShapeDtypeStruct((ROWS * PLANES, LANES), F32)
    early = pl.BlockSpec((256, LANES), lambda i, core: (0, 0))
    late = pl.BlockSpec((256, LANES), lambda i, core: (jnp.maximum(i, 1) - 1, 0))
    ins = [LINES, BOTH, early, late, early, late]
    return along(far_kernel, ins, [LINES] * 2, (out, out))(*args)


def solution(mesh):
    fine = Mesh(mesh.devices.reshape(8, 4, 2, 2, 2), ("z", "y", "xl", "xh", "c"))
    small_t, large_t = cross_strips()
    along_t = along_table()
    pair = [(0, 1), (1, 0)]

    def swap(message):
        return lax.all_to_all(message, ("z", "y", "xl"), split_axis=0, concat_axis=0, tiled=True)

    def shards(moments):
        grid = moments.shape
        own = moments.reshape(ROWS * PLANES, LANES)
        far_a = lax.ppermute(own[:256], "xh", pair)
        home = swap(pack(moments.reshape(ROWS, PLANES, LANES)).reshape(64, 9, 4, 128))
        home, far_a, own = lax.optimization_barrier((home, far_a, own))
        near = lax.ppermute(own, "c", pair)
        far_b = lax.ppermute(own[256:], "xh", pair)
        back = swap(cross(jnp.asarray(small_t), jnp.asarray(large_t), home).reshape(64, 72, 128))
        far_near_a = lax.ppermute(far_a, "c", pair)
        far_near_b = lax.ppermute(far_b, "c", pair)
        core = lax.axis_index("c").reshape(1)
        table = jnp.asarray(along_t)
        part = along_close(core, table, own, near)
        first_z, second_z = along_far(
            core, table, own, part, far_a, far_b, far_near_a, far_near_b
        )
        first_z, second_z, back = lax.optimization_barrier((first_z, second_z, back))
        first, second = unpack(back.reshape(4608, 128))
        return (
            first.reshape(grid),
            second.reshape(grid),
            first_z.reshape(grid),
            second_z.reshape(grid),
        )

    spec = P(("z", "y", "xl"), None, None, ("xh", "c"))
    return jax.shard_map(
        shards, mesh=fine, in_specs=(spec,), out_specs=(spec,) * 4, check_vma=False
    )
```

```python
import math

import jax
import jax.numpy as jnp
import ml_dtypes
import numpy as np
from jax import lax
from jax.experimental import pallas as pl
from jax.experimental.pallas import tpu as pltpu
from jax.sharding import Mesh
from jax.sharding import PartitionSpec as P

COUNT = 1536
HALF = COUNT // 2
QUARTER = COUNT // 4
ROWS = 24
LANES = 384
PLANES = 32
F32 = jnp.float32
BF16 = jnp.bfloat16


def kernels():
    k = np.arange(COUNT, dtype=np.float64)
    sign = np.where(np.arange(COUNT) % 2 == 0, 1.0, -1.0)
    angle = math.pi * np.where(k == 0, 1.0, k) / COUNT
    first = np.where(k == 0, 0.0, math.pi / COUNT * sign / np.tan(angle))
    second = np.where(
        k == 0,
        -math.pi**2 / 3 - (2 * math.pi / COUNT) ** 2 / 6,
        -sign * (2 * math.pi**2 / COUNT**2) / np.sin(angle) ** 2,
    )
    return first, second


def halves(table):
    high = table.astype(ml_dtypes.bfloat16)
    low = (table - high.astype(np.float64)).astype(ml_dtypes.bfloat16)
    return np.stack([high, low])


def cross_strips():
    def strip(block, value):
        gap = 2 * block + np.arange(block)[:, None] - np.arange(5 * block)[None, :]
        return halves(np.stack([value(d, gap) for d in kernels()]))

    def plus(d, gap):
        return (d[gap % COUNT] + d[(gap + HALF) % COUNT]) / 2

    both = strip(128, lambda d, gap: (plus(d, gap) + plus(d, gap + QUARTER)) / 2)
    cross = strip(128, lambda d, gap: (plus(d, gap) - plus(d, gap + QUARTER)) / 2)
    minus = strip(256, lambda d, gap: (d[gap % COUNT] - d[(gap + HALF) % COUNT]) / 2)
    return np.stack([both, cross]), minus


def along_table():
    cell = np.arange(LANES)
    blocks = [
        np.concatenate(
            [d[(cell[None, :] - cell[:, None] - LANES * r) % COUNT] for d in kernels()], axis=1
        )
        for r in range(4)
    ]
    return halves(np.stack(blocks))


def split(value):
    high = value.astype(BF16)
    return high, (value - high.astype(F32)).astype(BF16)


def three(left_high, left_low, right_high, right_low):
    total = jnp.dot(left_high, right_high, preferred_element_type=F32)
    total = total + jnp.dot(left_high, right_low, preferred_element_type=F32)
    return total + jnp.dot(left_low, right_high, preferred_element_type=F32)


def wide_three(left_high, left_low, right_high, right_low):
    both = jnp.concatenate([right_high, right_low], axis=1)
    width = right_high.shape[1]
    total = jnp.dot(left_high, both, preferred_element_type=F32)
    total = total[:, :width] + total[:, width:]
    return total + jnp.dot(left_low, right_high, preferred_element_type=F32)


def low_lanes(shape):
    return lax.broadcasted_iota(jnp.int32, shape, len(shape) - 1) < 64


def pack_kernel(x_hbm, msg_hbm, x_ref, msg_ref, in_sems, out_sems):
    gets = [
        pltpu.make_async_copy(x_hbm.at[:, 8 * g : 8 * g + 8], x_ref.at[g], in_sems.at[g])
        for g in range(4)
    ]
    puts = [
        pltpu.make_async_copy(msg_ref.at[g], msg_hbm.at[576 * g : 576 * g + 576], out_sems.at[g])
        for g in range(4)
    ]
    near = low_lanes((8, 128))
    for get in gets:
        get.start()
    for g in range(4):
        gets[g].wait()
        for i in range(ROWS):
            for low in range(2):
                at = pl.ds(36 * low + i, 8, stride=72)
                msg_ref[g, at, :] = x_ref[g, i, :, 128 * low : 128 * low + 128]
        for i in range(12):
            top, bottom = x_ref[g, i, :, 256:384], x_ref[g, i + 12, :, 256:384]
            lower = jnp.where(near, top, pltpu.roll(bottom, 64, 1))
            upper = jnp.where(near, pltpu.roll(top, 64, 1), bottom)
            msg_ref[g, pl.ds(24 + i, 8, stride=72), :] = lower
            msg_ref[g, pl.ds(60 + i, 8, stride=72), :] = upper
        puts[g].start()
    for put in puts:
        put.wait()


def pack(block):
    return pl.pallas_call(
        pack_kernel,
        in_specs=[pl.BlockSpec(memory_space=pltpu.HBM)],
        out_specs=pl.BlockSpec(memory_space=pltpu.HBM),
        out_shape=jax.ShapeDtypeStruct((2304, 128), F32),
        scratch_shapes=[
            pltpu.VMEM((4, ROWS, 8, LANES), F32),
            pltpu.VMEM((4, 576, 128), F32),
            pltpu.SemaphoreType.DMA((4,)),
            pltpu.SemaphoreType.DMA((4,)),
        ],
        compiler_params=pltpu.CompilerParams(vmem_limit_bytes=56 * 2**20),
    )(block)


def unpack_kernel(msg_ref, first_hbm, second_hbm, out_ref, sems):
    near = low_lanes((8, 128))
    puts = []
    for g in range(4):
        base = 1152 * g
        for d, (out_hbm, full, part) in enumerate(((first_hbm, 0, 24), (second_hbm, 48, 36))):
            for i in range(ROWS):
                for low in range(2):
                    at = pl.ds(base + 72 * low + full + i, 8, stride=144)
                    out_ref[d, g, i, :, 128 * low : 128 * low + 128] = msg_ref[at, :]
            for i in range(12):
                lower = msg_ref[pl.ds(base + part + i, 8, stride=144), :]
                upper = msg_ref[pl.ds(base + 72 + part + i, 8, stride=144), :]
                out_ref[d, g, i, :, 256:384] = jnp.where(near, lower, pltpu.roll(upper, 64, 1))
                out_ref[d, g, i + 12, :, 256:384] = jnp.where(
                    near, pltpu.roll(lower, 64, 1), upper
                )
            put = pltpu.make_async_copy(
                out_ref.at[d, g], out_hbm.at[:, 8 * g : 8 * g + 8], sems.at[2 * g + d]
            )
            put.start()
            puts.append(put)
    for put in puts:
        put.wait()


def unpack(message):
    out = jax.ShapeDtypeStruct((ROWS, PLANES, LANES), F32)
    return pl.pallas_call(
        unpack_kernel,
        in_specs=[pl.BlockSpec(memory_space=pltpu.VMEM)],
        out_specs=[pl.BlockSpec(memory_space=pltpu.HBM)] * 2,
        out_shape=(out, out),
        scratch_shapes=[
            pltpu.VMEM((2, 4, ROWS, 8, LANES), F32),
            pltpu.SemaphoreType.DMA((8,)),
        ],
        compiler_params=pltpu.CompilerParams(vmem_limit_bytes=16 * 2**20),
    )(message)


def cross_kernel(
    small_hbm,
    large_hbm,
    msg_hbm,
    out_hbm,
    small_strip,
    large_strip,
    small,
    msg,
    out,
    line,
    got_small,
    got_large,
    in_sems,
    table_sems,
    out_sems,
):
    gets = [
        pltpu.make_async_copy(msg_hbm.at[:, c], msg.at[c], in_sems.at[c]) for c in range(4)
    ]
    strips = [
        pltpu.make_async_copy(small_hbm, small_strip, table_sems.at[0]),
        pltpu.make_async_copy(large_hbm, large_strip, table_sems.at[1]),
    ]
    puts = [pltpu.make_async_copy(out.at[z], out_hbm.at[z], out_sems.at[z]) for z in range(8)]
    for copy in gets + strips:
        copy.start()

    for c in range(4):
        gets[c].wait()
        for y in range(4):
            at = 48 * (4 * c + y)
            top, bottom = msg[c, 0, y], msg[c, 1, y]
            for k, value in enumerate((top + bottom, top - bottom)):
                line[k, at : at + 24, 0:128] = value[0:24]
                line[k, at + 24 : at + 48, 0:128] = value[36:60]
                even, odd = value[24:36], value[60:72]
                parts = [even, pltpu.roll(even, 64, 1), odd, pltpu.roll(odd, 64, 1)]
                line[k, at : at + 48, 128:256] = jnp.concatenate(parts, axis=0)

    for copy in strips:
        copy.wait()
    for h in range(2):
        for d in range(2):
            for i in range(3):
                rows = slice(QUARTER * d + 128 * i, QUARTER * d + 128 * i + 128)
                lanes = slice(128 * (2 - i), 128 * (2 - i) + QUARTER)
                for k in range(2):
                    small[k, h, rows, :] = small_strip[k, h, d, :, lanes]
    head, tail = line[0, :QUARTER, :], line[0, QUARTER:, :]
    whole = head + tail
    whole = whole - jnp.sum(whole, axis=0, keepdims=True) * (1.0 / QUARTER)
    for k, value in enumerate((whole, head - tail)):
        high, low = split(value)
        got_small[k] = wide_three(small[k, 0], small[k, 1], high, low)

    high, low = split(line[1])
    near = low_lanes((12, 128))

    def products(i):
        for d in range(2):
            lanes = slice(256 * (2 - i), 256 * (2 - i) + HALF)
            left = large_strip[0, d, :, lanes], large_strip[1, d, :, lanes]
            got_large[HALF * d + 256 * i : HALF * d + 256 * i + 256, :] = wide_three(
                *left, high, low
            )

    def close(c):
        for y in range(4):
            for part_of in range(2):
                at = 48 * (4 * c + y) + ROWS * part_of
                for d, (full, part) in enumerate(((0, 24), (48, 36))):
                    minus = got_large[HALF * d + at : HALF * d + at + ROWS, :]
                    place = QUARTER * d + at % QUARTER
                    one = got_small[0, place : place + ROWS, :]
                    two = got_small[1, place : place + ROWS, :]
                    plus = one + two if at < QUARTER else one - two
                    for z, value in ((c, plus + minus), (c + 4, plus - minus)):
                        out[z, y, part_of, full : full + 24] = value[:, 0:128]
                        top, bottom = value[:12, 128:256], value[12:, 128:256]
                        out[z, y, part_of, part : part + 12] = jnp.where(
                            near, top, pltpu.roll(bottom, 64, 1)
                        )
        puts[c].start()
        puts[c + 4].start()

    products(0)
    products(1)
    close(0)
    products(2)
    close(1)
    close(2)
    close(3)
    for put in puts:
        put.wait()


def cross(small, large, message):
    return pl.pallas_call(
        cross_kernel,
        out_shape=jax.ShapeDtypeStruct((8, 4, 2, 72, 128), F32),
        in_specs=[
            pl.BlockSpec(memory_space=pltpu.HBM),
            pl.BlockSpec(memory_space=pltpu.HBM),
            pl.BlockSpec(memory_space=pl.ANY),
        ],
        out_specs=pl.BlockSpec(memory_space=pltpu.HBM),
        scratch_shapes=[
            pltpu.VMEM(small.shape, BF16),
            pltpu.VMEM(large.shape, BF16),
            pltpu.VMEM((2, 2, HALF, QUARTER), BF16),
            pltpu.VMEM((4, 2, 4, 72, 128), F32),
            pltpu.VMEM((8, 4, 2, 72, 128), F32),
            pltpu.VMEM((2, HALF, 256), F32),
            pltpu.VMEM((2, HALF, 256), F32),
            pltpu.VMEM((COUNT, 256), F32),
            pltpu.SemaphoreType.DMA((4,)),
            pltpu.SemaphoreType.DMA((2,)),
            pltpu.SemaphoreType.DMA((8,)),
        ],
        compiler_params=pltpu.CompilerParams(vmem_limit_bytes=60 * 2**20),
        cost_estimate=pl.CostEstimate(
            flops=3 * 2 * 3 * HALF * HALF * 256, bytes_accessed=12 * 2**20, transcendentals=0
        ),
    )(small, large, message.reshape(2, 4, 4, 72, 128))


def along_kernel(
    core_ref, table_ref, own, near, far_a, far_b, far_near_a, far_near_b, first_ref, second_ref
):
    core = core_ref[0]
    early = pl.program_id(0) == 0
    far = jnp.where(early, far_a[...], far_b[...])
    far_near = jnp.where(early, far_near_a[...], far_near_b[...])
    total = jnp.zeros((256, 2 * LANES), F32)
    pairs = ((own[...], 0), (near[...], 1 + 2 * core), (far, 2), (far_near, 3 - 2 * core))
    level = jnp.sum(own[...], axis=1, keepdims=True) * (1.0 / LANES)
    for block, r in pairs:
        high, low = split(block - level)
        total = total + three(high, low, table_ref[0, r], table_ref[1, r])
    first_ref[...] = total[:, :LANES]
    second_ref[...] = total[:, LANES:]


def along(core, table, *blocks):
    out = jax.ShapeDtypeStruct((ROWS * PLANES, LANES), F32)
    lines = pl.BlockSpec((256, LANES), lambda i, core: (i, 0))
    early = pl.BlockSpec((256, LANES), lambda i, core: (0, 0))
    late = pl.BlockSpec((256, LANES), lambda i, core: (jnp.maximum(i, 1) - 1, 0))
    return pl.pallas_call(
        along_kernel,
        grid_spec=pltpu.PrefetchScalarGridSpec(
            num_scalar_prefetch=1,
            grid=(3,),
            in_specs=[pl.BlockSpec((2, 4, LANES, 2 * LANES), lambda i, core: (0, 0, 0, 0))]
            + [lines, lines, early, late, early, late],
            out_specs=[lines] * 2,
        ),
        out_shape=(out, out),
        compiler_params=pltpu.CompilerParams(vmem_limit_bytes=24 * 2**20),
        cost_estimate=pl.CostEstimate(
            flops=2 * 3 * 768 * COUNT * 768, bytes_accessed=16 * 2**20, transcendentals=0
        ),
    )(core, table, *blocks)


def solution(mesh):
    fine = Mesh(mesh.devices.reshape(8, 4, 2, 2, 2), ("z", "y", "xl", "xh", "c"))
    small_t, large_t = cross_strips()
    along_t = along_table()
    pair = [(0, 1), (1, 0)]

    def swap(message):
        return lax.all_to_all(message, ("z", "y", "xl"), split_axis=0, concat_axis=0, tiled=True)

    def shards(moments):
        grid = moments.shape
        own = moments.reshape(ROWS * PLANES, LANES)
        far_a = lax.ppermute(own[:256], "xh", pair)
        near = lax.ppermute(own, "c", pair)
        home = swap(pack(moments.reshape(ROWS, PLANES, LANES)).reshape(64, 9, 4, 128))
        home, far_a, near = lax.optimization_barrier((home, far_a, near))
        far_b = lax.ppermute(own[256:], "xh", pair)
        back = swap(cross(jnp.asarray(small_t), jnp.asarray(large_t), home).reshape(64, 72, 128))
        far_near_a = lax.ppermute(far_a, "c", pair)
        far_near_b = lax.ppermute(far_b, "c", pair)
        core = lax.axis_index("c").reshape(1)
        first_z, second_z = along(
            core, jnp.asarray(along_t), own, near, far_a, far_b, far_near_a, far_near_b
        )
        first_z, second_z, back = lax.optimization_barrier((first_z, second_z, back))
        first, second = unpack(back.reshape(4608, 128))
        return (
            first.reshape(grid),
            second.reshape(grid),
            first_z.reshape(grid),
            second_z.reshape(grid),
        )

    spec = P(("z", "y", "xl"), None, None, ("xh", "c"))
    return jax.shard_map(
        shards, mesh=fine, in_specs=(spec,), out_specs=(spec,) * 4, check_vma=False
    )
```

```python
import math

import jax
import jax.numpy as jnp
import ml_dtypes
import numpy as np
from jax import lax
from jax.experimental import pallas as pl
from jax.experimental.pallas import tpu as pltpu
from jax.sharding import Mesh
from jax.sharding import PartitionSpec as P

COUNT = 1536
HALF = COUNT // 2
QUARTER = COUNT // 4
ROWS = 24
LANES = 384
PLANES = 32
F32 = jnp.float32
BF16 = jnp.bfloat16


def kernels():
    k = np.arange(COUNT, dtype=np.float64)
    sign = np.where(np.arange(COUNT) % 2 == 0, 1.0, -1.0)
    angle = math.pi * np.where(k == 0, 1.0, k) / COUNT
    first = np.where(k == 0, 0.0, math.pi / COUNT * sign / np.tan(angle))
    second = np.where(
        k == 0,
        -math.pi**2 / 3 - (2 * math.pi / COUNT) ** 2 / 6,
        -sign * (2 * math.pi**2 / COUNT**2) / np.sin(angle) ** 2,
    )
    return first, second


def halves(table):
    high = table.astype(ml_dtypes.bfloat16)
    low = (table - high.astype(np.float64)).astype(ml_dtypes.bfloat16)
    return np.stack([high, low])


def cross_strips():
    def strip(block, value):
        gap = 2 * block + np.arange(block)[:, None] - np.arange(5 * block)[None, :]
        return halves(np.stack([value(d, gap) for d in kernels()]))

    def plus(d, gap):
        return (d[gap % COUNT] + d[(gap + HALF) % COUNT]) / 2

    both = strip(128, lambda d, gap: (plus(d, gap) + plus(d, gap + QUARTER)) / 2)
    cross = strip(128, lambda d, gap: (plus(d, gap) - plus(d, gap + QUARTER)) / 2)
    minus = strip(256, lambda d, gap: (d[gap % COUNT] - d[(gap + HALF) % COUNT]) / 2)
    return np.stack([both, cross]), minus


def along_table():
    cell = np.arange(LANES)
    blocks = [
        np.concatenate(
            [d[(cell[None, :] - cell[:, None] - LANES * r) % COUNT] for d in kernels()], axis=1
        )
        for r in range(4)
    ]
    return halves(np.stack(blocks))


def split(value):
    high = value.astype(BF16)
    return high, (value - high.astype(F32)).astype(BF16)


def three(left_high, left_low, right_high, right_low):
    total = jnp.dot(left_high, right_high, preferred_element_type=F32)
    total = total + jnp.dot(left_high, right_low, preferred_element_type=F32)
    return total + jnp.dot(left_low, right_high, preferred_element_type=F32)


def wide_three(left_high, left_low, right_high, right_low):
    both = jnp.concatenate([right_high, right_low], axis=1)
    width = right_high.shape[1]
    total = jnp.dot(left_high, both, preferred_element_type=F32)
    total = total[:, :width] + total[:, width:]
    return total + jnp.dot(left_low, right_high, preferred_element_type=F32)


def low_lanes(shape):
    return lax.broadcasted_iota(jnp.int32, shape, len(shape) - 1) < 64


def pack_kernel(x_hbm, msg_hbm, x_ref, msg_ref, in_sems, out_sems):
    gets = [
        pltpu.make_async_copy(x_hbm.at[:, 8 * g : 8 * g + 8], x_ref.at[g], in_sems.at[g])
        for g in range(4)
    ]
    puts = [
        pltpu.make_async_copy(msg_ref.at[g], msg_hbm.at[576 * g : 576 * g + 576], out_sems.at[g])
        for g in range(4)
    ]
    near = low_lanes((8, 128))
    for get in gets:
        get.start()
    for g in range(4):
        gets[g].wait()
        for i in range(ROWS):
            for low in range(2):
                at = pl.ds(36 * low + i, 8, stride=72)
                msg_ref[g, at, :] = x_ref[g, i, :, 128 * low : 128 * low + 128]
        for i in range(12):
            top, bottom = x_ref[g, i, :, 256:384], x_ref[g, i + 12, :, 256:384]
            lower = jnp.where(near, top, pltpu.roll(bottom, 64, 1))
            upper = jnp.where(near, pltpu.roll(top, 64, 1), bottom)
            msg_ref[g, pl.ds(24 + i, 8, stride=72), :] = lower
            msg_ref[g, pl.ds(60 + i, 8, stride=72), :] = upper
        puts[g].start()
    for put in puts:
        put.wait()


def pack(block):
    return pl.pallas_call(
        pack_kernel,
        in_specs=[pl.BlockSpec(memory_space=pltpu.HBM)],
        out_specs=pl.BlockSpec(memory_space=pltpu.HBM),
        out_shape=jax.ShapeDtypeStruct((2304, 128), F32),
        scratch_shapes=[
            pltpu.VMEM((4, ROWS, 8, LANES), F32),
            pltpu.VMEM((4, 576, 128), F32),
            pltpu.SemaphoreType.DMA((4,)),
            pltpu.SemaphoreType.DMA((4,)),
        ],
        compiler_params=pltpu.CompilerParams(vmem_limit_bytes=56 * 2**20),
    )(block)


def unpack_kernel(msg_ref, first_hbm, second_hbm, out_ref, sems):
    near = low_lanes((8, 128))
    puts = []
    for g in range(4):
        base = 1152 * g
        for d, (out_hbm, full, part) in enumerate(((first_hbm, 0, 24), (second_hbm, 48, 36))):
            for i in range(ROWS):
                for low in range(2):
                    at = pl.ds(base + 72 * low + full + i, 8, stride=144)
                    out_ref[d, g, i, :, 128 * low : 128 * low + 128] = msg_ref[at, :]
            for i in range(12):
                lower = msg_ref[pl.ds(base + part + i, 8, stride=144), :]
                upper = msg_ref[pl.ds(base + 72 + part + i, 8, stride=144), :]
                out_ref[d, g, i, :, 256:384] = jnp.where(near, lower, pltpu.roll(upper, 64, 1))
                out_ref[d, g, i + 12, :, 256:384] = jnp.where(
                    near, pltpu.roll(lower, 64, 1), upper
                )
            put = pltpu.make_async_copy(
                out_ref.at[d, g], out_hbm.at[:, 8 * g : 8 * g + 8], sems.at[2 * g + d]
            )
            put.start()
            puts.append(put)
    for put in puts:
        put.wait()


def unpack(message):
    out = jax.ShapeDtypeStruct((ROWS, PLANES, LANES), F32)
    return pl.pallas_call(
        unpack_kernel,
        in_specs=[pl.BlockSpec(memory_space=pltpu.VMEM)],
        out_specs=[pl.BlockSpec(memory_space=pltpu.HBM)] * 2,
        out_shape=(out, out),
        scratch_shapes=[
            pltpu.VMEM((2, 4, ROWS, 8, LANES), F32),
            pltpu.SemaphoreType.DMA((8,)),
        ],
        compiler_params=pltpu.CompilerParams(vmem_limit_bytes=16 * 2**20),
    )(message)


def cross_kernel(
    small_hbm,
    large_hbm,
    msg_hbm,
    out_hbm,
    small_strip,
    large_strip,
    small,
    msg,
    out,
    line,
    got_small,
    got_large,
    in_sems,
    table_sems,
    out_sems,
):
    gets = [
        pltpu.make_async_copy(msg_hbm.at[:, c], msg.at[c], in_sems.at[c]) for c in range(4)
    ]
    strips = [
        pltpu.make_async_copy(small_hbm, small_strip, table_sems.at[0]),
        pltpu.make_async_copy(large_hbm, large_strip, table_sems.at[1]),
    ]
    puts = [pltpu.make_async_copy(out.at[z], out_hbm.at[z], out_sems.at[z]) for z in range(8)]
    for copy in gets + strips:
        copy.start()

    for c in range(4):
        gets[c].wait()
        for y in range(4):
            at = 48 * (4 * c + y)
            top, bottom = msg[c, 0, y], msg[c, 1, y]
            for k, value in enumerate((top + bottom, top - bottom)):
                line[k, at : at + 24, 0:128] = value[0:24]
                line[k, at + 24 : at + 48, 0:128] = value[36:60]
                even, odd = value[24:36], value[60:72]
                parts = [even, pltpu.roll(even, 64, 1), odd, pltpu.roll(odd, 64, 1)]
                line[k, at : at + 48, 128:256] = jnp.concatenate(parts, axis=0)

    for copy in strips:
        copy.wait()
    for h in range(2):
        for d in range(2):
            for i in range(3):
                rows = slice(QUARTER * d + 128 * i, QUARTER * d + 128 * i + 128)
                lanes = slice(128 * (2 - i), 128 * (2 - i) + QUARTER)
                for k in range(2):
                    small[k, h, rows, :] = small_strip[k, h, d, :, lanes]
    head, tail = line[0, :QUARTER, :], line[0, QUARTER:, :]
    whole = head + tail
    whole = whole - jnp.sum(whole, axis=0, keepdims=True) * (1.0 / QUARTER)
    for k, value in enumerate((whole, head - tail)):
        high, low = split(value)
        got_small[k] = wide_three(small[k, 0], small[k, 1], high, low)

    high, low = split(line[1])
    near = low_lanes((12, 128))

    def products(i):
        for d in range(2):
            lanes = slice(256 * (2 - i), 256 * (2 - i) + HALF)
            left = large_strip[0, d, :, lanes], large_strip[1, d, :, lanes]
            got_large[HALF * d + 256 * i : HALF * d + 256 * i + 256, :] = wide_three(
                *left, high, low
            )

    def close(c):
        for y in range(4):
            for part_of in range(2):
                at = 48 * (4 * c + y) + ROWS * part_of
                for d, (full, part) in enumerate(((0, 24), (48, 36))):
                    minus = got_large[HALF * d + at : HALF * d + at + ROWS, :]
                    place = QUARTER * d + at % QUARTER
                    one = got_small[0, place : place + ROWS, :]
                    two = got_small[1, place : place + ROWS, :]
                    plus = one + two if at < QUARTER else one - two
                    for z, value in ((c, plus + minus), (c + 4, plus - minus)):
                        out[z, y, part_of, full : full + 24] = value[:, 0:128]
                        top, bottom = value[:12, 128:256], value[12:, 128:256]
                        out[z, y, part_of, part : part + 12] = jnp.where(
                            near, top, pltpu.roll(bottom, 64, 1)
                        )
        puts[c].start()
        puts[c + 4].start()

    products(0)
    products(1)
    close(0)
    products(2)
    close(1)
    close(2)
    close(3)
    for put in puts:
        put.wait()


def cross(small, large, message):
    return pl.pallas_call(
        cross_kernel,
        out_shape=jax.ShapeDtypeStruct((8, 4, 2, 72, 128), F32),
        in_specs=[
            pl.BlockSpec(memory_space=pltpu.HBM),
            pl.BlockSpec(memory_space=pltpu.HBM),
            pl.BlockSpec(memory_space=pl.ANY),
        ],
        out_specs=pl.BlockSpec(memory_space=pltpu.HBM),
        scratch_shapes=[
            pltpu.VMEM(small.shape, BF16),
            pltpu.VMEM(large.shape, BF16),
            pltpu.VMEM((2, 2, HALF, QUARTER), BF16),
            pltpu.VMEM((4, 2, 4, 72, 128), F32),
            pltpu.VMEM((8, 4, 2, 72, 128), F32),
            pltpu.VMEM((2, HALF, 256), F32),
            pltpu.VMEM((2, HALF, 256), F32),
            pltpu.VMEM((COUNT, 256), F32),
            pltpu.SemaphoreType.DMA((4,)),
            pltpu.SemaphoreType.DMA((2,)),
            pltpu.SemaphoreType.DMA((8,)),
        ],
        compiler_params=pltpu.CompilerParams(vmem_limit_bytes=60 * 2**20),
        cost_estimate=pl.CostEstimate(
            flops=3 * 2 * 3 * HALF * HALF * 256, bytes_accessed=12 * 2**20, transcendentals=0
        ),
    )(small, large, message.reshape(2, 4, 4, 72, 128))


def add_lines(total, table_ref, pairs, level):
    for block, r in pairs:
        high, low = split(block - level)
        total = total + three(high, low, table_ref[0, r], table_ref[1, r])
    return total


def line_level(own):
    return jnp.sum(own[...], axis=1, keepdims=True) * (1.0 / LANES)


def close_kernel(core_ref, table_ref, own, near, out_ref):
    pairs = ((own[...], 0), (near[...], 1 + 2 * core_ref[0]))
    total = jnp.zeros((256, 2 * LANES), F32)
    out_ref[...] = add_lines(total, table_ref, pairs, line_level(own))


def far_kernel(
    core_ref, table_ref, own, part, far_a, far_b, far_near_a, far_near_b, first_ref, second_ref
):
    early = pl.program_id(0) == 0
    far = jnp.where(early, far_a[...], far_b[...])
    far_near = jnp.where(early, far_near_a[...], far_near_b[...])
    pairs = ((far, 2), (far_near, 3 - 2 * core_ref[0]))
    total = add_lines(part[...], table_ref, pairs, line_level(own))
    first_ref[...] = total[:, :LANES]
    second_ref[...] = total[:, LANES:]


LINES = pl.BlockSpec((256, LANES), lambda i, core: (i, 0))
BOTH = pl.BlockSpec((256, 2 * LANES), lambda i, core: (i, 0))


def along(kernel, ins, outs, shapes):
    return pl.pallas_call(
        kernel,
        grid_spec=pltpu.PrefetchScalarGridSpec(
            num_scalar_prefetch=1,
            grid=(3,),
            in_specs=[pl.BlockSpec((2, 4, LANES, 2 * LANES), lambda i, core: (0, 0, 0, 0))] + ins,
            out_specs=outs,
        ),
        out_shape=shapes,
        compiler_params=pltpu.CompilerParams(vmem_limit_bytes=24 * 2**20),
        cost_estimate=pl.CostEstimate(
            flops=3 * 768 * COUNT * 768, bytes_accessed=12 * 2**20, transcendentals=0
        ),
    )


def along_close(*args):
    shape = jax.ShapeDtypeStruct((ROWS * PLANES, 2 * LANES), F32)
    return along(close_kernel, [LINES, LINES], BOTH, shape)(*args)


def along_far(*args):
    out = jax.ShapeDtypeStruct((ROWS * PLANES, LANES), F32)
    early = pl.BlockSpec((256, LANES), lambda i, core: (0, 0))
    late = pl.BlockSpec((256, LANES), lambda i, core: (jnp.maximum(i, 1) - 1, 0))
    ins = [LINES, BOTH, early, late, early, late]
    return along(far_kernel, ins, [LINES] * 2, (out, out))(*args)


def solution(mesh):
    fine = Mesh(mesh.devices.reshape(8, 4, 2, 2, 2), ("z", "y", "xl", "xh", "c"))
    small_t, large_t = cross_strips()
    along_t = along_table()
    pair = [(0, 1), (1, 0)]

    def swap(message):
        return lax.all_to_all(message, ("z", "y", "xl"), split_axis=0, concat_axis=0, tiled=True)

    def shards(moments):
        grid = moments.shape
        own = moments.reshape(ROWS * PLANES, LANES)
        far_a = lax.ppermute(own[:256], "xh", pair)
        near = lax.ppermute(own, "c", pair)
        home = swap(pack(moments.reshape(ROWS, PLANES, LANES)).reshape(64, 9, 4, 128))
        home, far_a, near = lax.optimization_barrier((home, far_a, near))
        far_b = lax.ppermute(own[256:], "xh", pair)
        back = swap(cross(jnp.asarray(small_t), jnp.asarray(large_t), home).reshape(64, 72, 128))
        far_near_a = lax.ppermute(far_a, "c", pair)
        far_near_b = lax.ppermute(far_b, "c", pair)
        core = lax.axis_index("c").reshape(1)
        table = jnp.asarray(along_t)
        part = along_close(core, table, own, near)
        first_z, second_z = along_far(
            core, table, own, part, far_a, far_b, far_near_a, far_near_b
        )
        first_z, second_z, back = lax.optimization_barrier((first_z, second_z, back))
        first, second = unpack(back.reshape(4608, 128))
        return (
            first.reshape(grid),
            second.reshape(grid),
            first_z.reshape(grid),
            second_z.reshape(grid),
        )

    spec = P(("z", "y", "xl"), None, None, ("xh", "c"))
    return jax.shard_map(
        shards, mesh=fine, in_specs=(spec,), out_specs=(spec,) * 4, check_vma=False
    )
```
